512 devices in a mesh: seq: 128 (over z, y, core), mp: 2 (over x_lo), dp: 2 (over x_hi).
Axes of the slice: x: 4 (x_hi: 2, x_lo: 2; x = x_hi * 2 + x_lo), y: 8, z: 8, core: 2. Of those that a mesh axis runs over, the one named last changes fastest.
Arguments:
- byte_rows: bfloat16 [65536, 1280], P(('dp', 'seq')), parts along dimension 0, may hold values from -6 to 6
- norm_gain: float32 [1280], replicated, may hold values from 0.1 to 1.9
- key_weight: bfloat16 [1280, 512], P('seq', 'mp'), may hold values from -0.15625 to 0.15625
- value_weight: bfloat16 [1280, 3072], P('seq', 'mp'), may hold values from -0.15625 to 0.15625
- pool_query: float32 [4, 128], P('mp'), may hold values from -320 to 320
- patch_starts: int32 [8192], P(('dp', 'seq')), parts along dimension 0, may hold values from 0 to 32767, as said below
Outputs:
- patch_mix: bfloat16 [8192, 2048], P(('dp', 'seq'), 'mp'), parts along dimension 0
The draws below stay inside these ranges and needn't reach their ends.
There are 2 independent parts, one for each index of `dp`. The reference program is written for one: setup_inputs(seed, part) draws one part's arguments, and reference() takes and returns one part's arrays. A program takes and returns all parts, laid end to end along the dimension named above; an argument that names none is the same for every part. Nothing has to cross between parts.
Inputs may be any that keep to these rules, and one draw needn't show every extreme that they name: Sorted and distinct. The bytes fall into aligned blocks of 1024 bytes (the bytes of 4 neighbouring indices of seq, starting at index 0); each block holds exactly 128 patches, the first starting at the block's first byte. Patch p covers the bytes from patch_starts[p] to the next start minus 1 (the last patch to 32767). No patch is longer than 256 bytes, and each block holds a patch of exactly 256 bytes.
All inputs are finite; a program needn't handle non-finite values.
Results may differ from the reference program's by a relative error of at most 0.014.
Values may be sent and summed in bfloat16 or wider, within the bound.
A program may use at most 64 MiB of HBM per device.

```python
import math
import jax
import jax.numpy as jnp
from jax import lax

DE = 1280
DH = 128
KVH = 4
GQ = 4
BYTE_DEV = 256
PATCH_DEV = 32
BYTES = 32768
PATCHES = 4096
VW = 768


def draw_patch_starts(key, part):
    key = jax.random.fold_in(key, 11)
    block_bytes = 4 * BYTE_DEV
    block_patches = 4 * PATCH_DEV
    block_total = BYTES // block_bytes
    half_slab = BYTE_DEV // 2

    def one_block(block_key):
        key_long, key_dense, key_score = jax.random.split(block_key, 3)
        long_slab = jax.random.randint(key_long, (), 0, 3)
        dense_slab = jax.random.randint(key_dense, (), 0, 4)
        spots = jnp.arange(block_bytes, dtype=jnp.int32)
        forced = (spots == 0) | (spots >= half_slab) & ((spots - half_slab) % BYTE_DEV == 0)
        lower_edge = half_slab + BYTE_DEV * long_slab
        excluded = (spots > lower_edge) & (spots < lower_edge + BYTE_DEV)
        dense = spots // BYTE_DEV == dense_slab
        raw_score = jax.random.randint(key_score, (block_bytes,), 0, 65536)
        raw_score = jnp.where(dense, 32768 + raw_score // 2, raw_score)
        scored = raw_score * block_bytes + spots
        scored = jnp.where(forced, 1073741824 + spots, jnp.where(excluded, -1 - spots, scored))
        picked = lax.top_k(scored, block_patches)[1]
        return jnp.sort(picked).astype(jnp.int32)
    starts = jax.vmap(one_block)(jax.random.split(key, block_total))
    offsets = (jnp.arange(block_total, dtype=jnp.int32) * block_bytes)[:, None]
    return (starts + offsets).reshape(-1).astype(jnp.int32)


def draw_pool_query(key, part):
    key = jax.random.fold_in(key, 23)
    key_entries = jax.random.fold_in(key, 0)
    entries = jax.random.normal(key_entries, (KVH, DH), jnp.float32)
    return jnp.clip(entries, -4.0, 4.0) * 2.0


def block_scale(key, dims, pieces, least, high):
    factor_of, own = 1.0, jax.random.fold_in(key, 6)
    for axis_at, blocks in pieces:
        steps = jnp.exp(jax.random.uniform(jax.random.fold_in(own, axis_at), (blocks,), jnp.float32, least / len(pieces), high / len(pieces)))
        factor_of = factor_of * jnp.repeat(steps, dims[axis_at] // blocks).reshape([-1 if axis == axis_at else 1 for axis in range(len(dims))])
    return factor_of


def bell_draw(own_key, extent, spread, most, cuts=(), held_as=jnp.bfloat16):
    level = block_scale(own_key, extent, cuts, -0.22, 0.18) if cuts else 1.0
    values = jax.random.normal(own_key, extent, jnp.float32) * spread * level
    return jnp.minimum(jnp.maximum(values, -most), most).astype(held_as)


def setup_inputs(seed: int = 0, part: int = 0) -> dict:
    key_of = jax.random.split(jax.random.key(seed), 7)
    part_keys = jax.random.split(jax.random.fold_in(key_of[6], part), 7)
    byte_rows = bell_draw(part_keys[0], (BYTES, DE), 1.0, 6.0, ((0, 128),))
    norm_gain = jnp.clip(1.0 + 0.18 * jax.random.normal(key_of[1], (DE,), jnp.float32), 0.1, 1.9)
    key_weight = bell_draw(key_of[2], (DE, KVH * DH), DE ** -0.5, 0.15625, ((0, 128), (1, 2)))
    value_weight = bell_draw(key_of[3], (DE, KVH * VW), DE ** -0.5, 0.15625, ((0, 128), (1, 2)))
    pool_query = draw_pool_query(jax.random.fold_in(key_of[6], 71), part)
    patch_starts = draw_patch_starts(jax.random.fold_in(jax.random.fold_in(key_of[6], part), 71), part)
    return {"byte_rows": byte_rows, "norm_gain": norm_gain, "key_weight": key_weight, "value_weight": value_weight, "pool_query": pool_query, "patch_starts": patch_starts}


def reference(byte_rows, norm_gain, key_weight, value_weight, pool_query, patch_starts):
    widened = byte_rows.astype(jnp.float32)
    scale_row = lax.rsqrt(lax.optimization_barrier(jnp.mean(widened * widened, axis=-1, keepdims=True)) + 1e-05)
    normed = (widened * scale_row * norm_gain).astype(jnp.bfloat16)
    byte_keys = jnp.dot(normed, key_weight, preferred_element_type=jnp.float32).reshape(BYTES, KVH, DH)
    byte_values = jnp.dot(normed, value_weight, preferred_element_type=jnp.float32).astype(jnp.bfloat16).reshape(BYTES, KVH, VW)
    pool_scores = jnp.einsum('bgd,gd->bg', byte_keys, pool_query, precision=lax.Precision.HIGHEST) / math.sqrt(DH)
    block_bytes = 4 * BYTE_DEV
    block_patches = 4 * PATCH_DEV

    def pool_block(block_number):
        first_byte = (block_number * block_bytes).astype(jnp.int32)
        first_patch = (block_number * block_patches).astype(jnp.int32)
        block_starts = lax.dynamic_slice_in_dim(patch_starts, first_patch, block_patches)
        positions = first_byte + jnp.arange(block_bytes, dtype=jnp.int32)
        segment = lax.optimization_barrier(jnp.sum((block_starts[:, None] <= positions[None, :]).astype(jnp.int32), axis=0)) - 1
        member = segment[None, :] == jnp.arange(block_patches, dtype=jnp.int32)[:, None]
        scores_here = lax.dynamic_slice_in_dim(pool_scores, first_byte, block_bytes, 0)
        values_here = lax.dynamic_slice_in_dim(byte_values, first_byte, block_bytes, 0)
        masked = jnp.where(member[:, :, None], scores_here[None, :, :], -1e+30)
        patch_top = lax.optimization_barrier(jnp.max(masked, axis=1))
        pool_weights = jnp.where(member[:, :, None], jnp.exp(masked - patch_top[:, None, :]), 0.0).astype(jnp.bfloat16)
        pool_total = lax.optimization_barrier(jnp.sum(pool_weights.astype(jnp.float32), axis=1))
        pool_sum = jnp.einsum('jbg,bgc->jgc', pool_weights.astype(jnp.float32), values_here.astype(jnp.float32))
        return (pool_sum / pool_total[:, :, None]).astype(jnp.bfloat16)
    block_total = BYTES // block_bytes
    pooled = lax.map(pool_block, jnp.arange(block_total, dtype=jnp.int32)).reshape(PATCHES, KVH, VW)
    query_width = GQ * DH
    queries = pooled[:, :, :query_width].reshape(PATCHES, KVH, GQ, DH)
    patch_keys = pooled[:, :, query_width:query_width + DH]
    patch_values = pooled[:, :, query_width + DH:]
    block_rows = math.gcd(PATCHES, 512)

    def attend(block_number):
        first_row = (block_number * block_rows).astype(jnp.int32)
        query_block = lax.dynamic_slice_in_dim(queries, first_row, block_rows, 0).astype(jnp.float32)
        logits = jnp.einsum('pghd,kgd->pghk', query_block, patch_keys.astype(jnp.float32)) / math.sqrt(DH)
        query_positions = first_row + jnp.arange(block_rows, dtype=jnp.int32)
        key_positions = jnp.arange(PATCHES, dtype=jnp.int32)
        causal = key_positions[None, :] <= query_positions[:, None]
        logits = jnp.where(causal[:, None, None, :], logits, -1e+30)
        highest = lax.optimization_barrier(jnp.max(logits, axis=-1, keepdims=True))
        raised = jnp.exp(logits - highest)
        attention = (raised / lax.optimization_barrier(jnp.sum(raised, axis=-1, keepdims=True))).astype(jnp.bfloat16)
        mixed_rows = jnp.einsum('pghk,kgd->pghd', attention.astype(jnp.float32), patch_values.astype(jnp.float32))
        return mixed_rows.astype(jnp.bfloat16).reshape(block_rows, KVH * GQ * DH)
    row_blocks = PATCHES // block_rows
    mixed_all = lax.map(attend, jnp.arange(row_blocks, dtype=jnp.int32))
    return mixed_all.reshape(PATCHES, KVH * GQ * DH)
```

```python
import functools
import math

import jax
import jax.numpy as jnp
from jax import lax
from jax.experimental import pallas as pl
from jax.experimental.pallas import tpu as pltpu
from jax.sharding import PartitionSpec as P

DH = 128
GQ = 4
VW = 768
HALF = 32
LANES = 256
NEG = -1e30
MESH = pl.DeviceIdType.MESH
f32 = jnp.float32
bf16 = jnp.bfloat16


def iota(shape, dim):
    return lax.broadcasted_iota(jnp.int32, shape, dim)


def dot(a, b, dims=((1,), (0,))):
    return lax.dot_general(a, b, (dims, ((), ())), preferred_element_type=f32)


def kernel(
    side,
    bytes_ref,
    gain_ref,
    kw_ref,
    vw_ref,
    pq_ref,
    starts_ref,
    out_ref,
    wbuf,
    kvbuf,
    wstage,
    sib_bytes,
    normed,
    starts_buf,
    key_stage,
    key_recv,
    key_z,
    key_y,
    send_rows,
    own_rows,
    got_rows,
    send_stats,
    got_stats,
    spread,
    top_ref,
    total_ref,
    mix_ref,
    out_send,
    out_got,
    w_recv,
    kv_recv,
    sib_recv,
    starts_recv,
    keyz_recv,
    keyy_recv,
    pair_recv,
    out_recv,
    w_send,
    kv_send,
    sib_send,
    starts_send,
    keyz_send,
    keyy_send,
    pair_send,
    out_send_sem,
):
    me = lax.axis_index("seq")
    core = lax.rem(me, 2)
    y = lax.rem(me // 2, side)
    z = me // (2 * side)
    chip = me // 2
    block_at = lax.rem(me, 4)
    pair_at = lax.rem(chip, 2)
    width = bytes_ref.shape[1]
    rows = bytes_ref.shape[0]

    def at(zz, yy, cc):
        return (zz * side + yy) * 2 + cc

    sibling = at(z, y, 1 - core)
    pair_y = y + 1 - 2 * pair_at
    pair = at(z, pair_y, core)
    cross = at(z, pair_y, 1 - core)

    def wrap(index):
        return lax.rem(index + 2 * side, side)

    def copy(src, dst, send_sem, recv_sem, target):
        return pltpu.make_async_remote_copy(
            src_ref=src,
            dst_ref=dst,
            send_sem=send_sem,
            recv_sem=recv_sem,
            device_id={"seq": target},
            device_id_type=MESH,
        )

    def arrived(ref, sem):
        pltpu.make_async_copy(ref, ref, sem).wait()

    barrier = pltpu.get_barrier_semaphore()

    def greet(target):
        pl.semaphore_signal(barrier, inc=1, device_id={"seq": target}, device_id_type=MESH)

    @pl.loop(1, side)
    def _(i):
        greet(at(wrap(z + i), y, core))
        greet(at(z, wrap(y + i), core))

    greet(sibling)
    greet(cross)

    part = vw_ref[...].astype(f32)
    depth = part.shape[0]
    pieces = []
    for head in range(2):
        cuts = [part[:, head * VW + n * LANES : head * VW + (n + 1) * LANES] for n in range(VW // LANES)]
        cuts.append(jnp.zeros((HALF - depth * len(cuts), LANES), f32))
        pieces.append(jnp.concatenate(cuts, axis=0).astype(bf16))
    first_core = core == 0
    wbuf[z, y, core] = jnp.where(first_core, pieces[0], pieces[1])
    wstage[...] = jnp.where(first_core, pieces[1], pieces[0])

    folded = kw_ref[...].astype(f32)
    row_at = iota((depth, 128), 0)
    lane_at = iota((depth, 128), 1)
    keyed = []
    for head in range(2):
        col = jnp.sum(folded[:, head * DH : (head + 1) * DH] * pq_ref[head : head + 1, :], axis=1, keepdims=True)
        keyed.append(jnp.sum(jnp.where(lane_at == row_at + core * 16, col, 0.0), axis=0, keepdims=True))
    key_stage[0] = jnp.where(first_core, keyed[1], keyed[0])
    key_own = jnp.where(first_core, keyed[0], keyed[1])

    starts_buf[block_at] = jnp.concatenate(
        [starts_ref[...], jnp.zeros((1, 128 - starts_ref.shape[1]), jnp.int32)], axis=1
    )

    pl.semaphore_wait(barrier, 2 * side)

    to_sibling = [
        copy(key_stage, key_recv, sib_send.at[0], sib_recv.at[0], sibling),
        copy(wstage, wbuf.at[z, y, core], sib_send.at[1], sib_recv.at[1], sibling),
        copy(bytes_ref, sib_bytes, sib_send.at[2], sib_recv.at[2], sibling),
    ]
    for one in to_sibling:
        one.start()
    to_block = [
        copy(starts_buf.at[block_at], starts_buf.at[block_at], starts_send.at[k], starts_recv.at[block_at], target)
        for k, target in enumerate((sibling, pair, cross))
    ]
    for one in to_block:
        one.start()

    def ref_of(buf, half, a, b):
        return buf.at[a, b, 0] if half == 0 else buf.at[b, a, 1]

    def dev_of(half, a, b):
        return at(a, b, core) if half == 0 else at(b, a, core)

    def own_of(half):
        return (z, y) if half == 0 else (y, z)

    def sem_of(sems, half, a, b):
        return sems.at[a, b, 0] if half == 0 else sems.at[b, a, 1]

    def ring(buf, recv, send, half, a, b, step):
        a0, b0 = own_of(half)
        ref = ref_of(buf, half, a, b)
        copy(
            ref, ref, send.at[half, 1], sem_of(recv, half, a, b), dev_of(half, a0, wrap(b0 + step))
        ).start()

    def pass_on(buf, recv, send, half, a, b, step, distance, even):
        last = distance == side // 2 - 1
        if not last or even == (step == 1):
            ring(buf, recv, send, half, a, b, step)

    def begin(buf, recv, send, half):
        a0, b0 = own_of(half)
        ref = ref_of(buf, half, a0, b0)
        for step in (1, -1):
            pass_on(buf, recv, send, half, a0, b0, step, 0, True)

        @pl.loop(1, side)
        def _(i):
            copy(
                ref, ref, send.at[half, 0], sem_of(recv, half, a0, b0), dev_of(half, wrap(a0 + i), b0)
            ).start()

    def visit(buf, recv, send, distance, t):
        for half in (0, 1):
            a0, b0 = own_of(half)
            for even, a in ((True, wrap(a0 - t)), (False, wrap(a0 + t + 1))):
                if distance == 0:

                    def take(half=half, a=a, b0=b0, even=even):
                        arrived(ref_of(buf, half, a, b0), sem_of(recv, half, a, b0))
                        for step in (1, -1):
                            pass_on(buf, recv, send, half, a, b0, step, 0, even)

                    if even:
                        pl.when(t > 0)(take)
                    else:
                        take()
                elif distance < side // 2:
                    for step in (1, -1):
                        b = wrap(b0 - step * distance)
                        arrived(ref_of(buf, half, a, b), sem_of(recv, half, a, b))
                        pass_on(buf, recv, send, half, a, b, step, distance, even)
                else:
                    b = wrap(b0 + distance)
                    arrived(ref_of(buf, half, a, b), sem_of(recv, half, a, b))

    def stage(buf, recv, send, distance):
        @pl.loop(0, side // 2)
        def _(t):
            visit(buf, recv, send, distance, t)

    def sent(buf, send):
        for half in (0, 1):
            ref = buf.at[0, pl.ds(0, side - 1), half]
            arrived(ref, send.at[half, 0])
            ref = buf.at[:, pl.ds(0, side - 1), half]
            arrived(ref, send.at[half, 1])

    weights = (wbuf, w_recv, w_send)
    sib_piece = wbuf.at[z, y, 1 - core]

    @pl.when(first_core)
    def _():
        begin(*weights, 0)
        arrived(sib_piece, sib_recv.at[1])
        begin(*weights, 1)

    @pl.when(core == 1)
    def _():
        begin(*weights, 1)
        arrived(sib_piece, sib_recv.at[1])
        begin(*weights, 0)

    arrived(key_recv, sib_recv.at[0])
    key_z[z] = key_own + key_recv[0]

    @pl.loop(1, side)
    def _(i):
        copy(key_z.at[z], key_z.at[z], keyz_send, keyz_recv.at[z], at(wrap(z + i), y, core)).start()

    def norm_rows(ref, first):
        @pl.loop(0, rows // 32)
        def _(i):
            at_row = pl.multiple_of(i * 32, 32)
            wide = ref[pl.ds(at_row, 32), :].astype(f32)
            scale = lax.rsqrt(jnp.mean(wide * wide, axis=-1, keepdims=True) + 1e-05)
            normed[pl.ds(pl.multiple_of(first + at_row, 32), 32), :] = (wide * scale * gain_ref[...]).astype(bf16)

    norm_rows(bytes_ref, core * rows)

    @pl.loop(1, side)
    def _(i):
        other = wrap(z + i)
        arrived(key_z.at[other], keyz_recv.at[other])

    key_y[y] = jnp.concatenate([key_z[i] for i in range(side)], axis=0)

    @pl.loop(1, side)
    def _(i):
        copy(key_y.at[y], key_y.at[y], keyy_send, keyy_recv.at[y], at(z, wrap(y + i), core)).start()

    stage(*weights, 0)
    arrived(sib_bytes, sib_recv.at[2])
    norm_rows(sib_bytes, (1 - core) * rows)
    if side > 2:
        stage(*weights, 1)

    @pl.loop(1, side)
    def _(i):
        other = wrap(y + i)
        arrived(key_y.at[other], keyy_recv.at[other])

    chips = side * side
    table = key_y[...].reshape(chips, 128)
    high = table.astype(bf16).astype(f32)
    middle = (table - high).astype(bf16).astype(f32)
    low = (table - high - middle).astype(bf16).astype(f32)
    packed = (high + pltpu.roll(middle, 32, axis=1) + pltpu.roll(low, 64, axis=1)).astype(bf16)
    column = iota((1, width), 1)
    column_chip = column // (2 * depth)
    column_row = lax.rem(column_chip, side) * side + column_chip // side
    pick = jnp.where(iota((chips, width), 0) == column_row, 1.0, 0.0).astype(bf16)
    taken = dot(packed, pick, ((0,), (0,)))
    column_lane = lax.rem(column // depth, 2) * 16 + lax.rem(column, depth)
    lane_row = iota((128, width), 0)
    key_rows = jnp.where(lax.rem(lane_row, 32) == column_lane, taken, 0.0).astype(bf16)
    scores = jnp.sum(dot(key_rows, normed[...], ((1,), (1,))), axis=0, keepdims=True) / math.sqrt(DH)

    for k in range(1, 4):
        other = lax.rem(block_at + k, 4)
        arrived(starts_buf.at[other], starts_recv.at[other])
    patch_sub = iota((HALF, 128), 0)
    patch_lane = iota((HALF, 128), 1)
    first_cols, next_cols = [], []
    for q in range(4):
        row = starts_buf[q]
        follow = (chip // 2 + 1) * (4 * rows) if q == 3 else starts_buf[q + 1][:, 0:1]
        row = jnp.where(iota((1, 128), 1) == HALF, follow, row)
        first_cols.append(jnp.sum(jnp.where(patch_lane == patch_sub, row, 0), axis=1, keepdims=True))
        next_cols.append(jnp.sum(jnp.where(patch_lane == patch_sub + 1, row, 0), axis=1, keepdims=True))
    first_col = jnp.concatenate(first_cols, axis=0)
    next_col = jnp.concatenate(next_cols, axis=0)
    position = chip * (2 * rows) + iota((1, 2 * rows), 1)
    member = (first_col <= position) & (position < next_col)

    masked = jnp.where(member, scores, NEG)
    top = jnp.max(masked, axis=1, keepdims=True)
    weight = jnp.where(member, jnp.exp(masked - top), 0.0).astype(bf16)
    total = jnp.sum(weight.astype(f32), axis=1, keepdims=True)
    share = jnp.where(total > 0.0, 1.0 / jnp.maximum(total, 1e-30), 0.0)
    pooled_rows = dot(weight, normed[...]) * share
    half_rows = 2 * HALF
    own_rows[...] = pooled_rows.reshape(2, half_rows, width)
    send_rows[...] = pooled_rows.astype(bf16).reshape(2, half_rows, width)
    eye = iota((4 * HALF, 128), 0) == iota((4 * HALF, 128), 1)
    top_row = jnp.sum(jnp.where(eye, top, 0.0), axis=0, keepdims=True)
    total_row = jnp.sum(jnp.where(eye, total, 0.0), axis=0, keepdims=True)
    stats = jnp.concatenate([top_row, total_row, jnp.zeros((6, 128), f32)], axis=0)
    send_stats[...] = stats
    to_pair = [
        copy(send_rows.at[1 - pair_at], got_rows, pair_send.at[0], pair_recv.at[0], pair),
        copy(send_stats, got_stats, pair_send.at[1], pair_recv.at[1], pair),
    ]
    for one in to_pair:
        one.start()

    for distance in range(2, side // 2):
        stage(*weights, distance)

    for one in to_pair:
        one.wait_recv()
    eye = iota((half_rows, 128), 1) == iota((half_rows, 128), 0) + pair_at * half_rows

    def to_column(row):
        return jnp.sum(jnp.where(eye, row, 0.0), axis=1, keepdims=True)

    own_top, own_total = to_column(send_stats[0:1, :]), to_column(send_stats[1:2, :])
    got_top, got_total = to_column(got_stats[0:1, :]), to_column(got_stats[1:2, :])
    top = jnp.maximum(own_top, got_top)
    own_part = jnp.exp(own_top - top) * own_total
    got_part = jnp.exp(got_top - top) * got_total
    share = 1.0 / (own_part + got_part)
    merged = own_rows[pair_at] * (own_part * share) + got_rows[...].astype(f32) * (got_part * share)
    merged = merged.astype(bf16)

    lane = iota((1, 128), 1)
    in_piece = lax.rem(lane, HALF)
    which = in_piece // depth
    source = jnp.where(in_piece < 3 * depth, (lane // HALF) * depth + lax.rem(in_piece, depth), -100000)
    window = min(256, width)
    sub = iota((window, 128), 0)
    for b in range(wbuf.shape[0] * side * 2 * HALF // 128):
        left = min(4 * depth * b // 128 * 128, width - window)
        choose = jnp.where(sub == source + (4 * depth * b - left), 1.0, 0.0).astype(bf16)
        block = dot(merged[:, left : left + window], choose)
        for n in range(3):
            spread[n * half_rows : (n + 1) * half_rows, b * 128 : (b + 1) * 128] = jnp.where(
                which == n, block, 0.0
            ).astype(bf16)

    stage(*weights, side // 2)
    mapped = jnp.zeros((3 * half_rows, LANES), f32)
    span = side * 2 * HALF
    for zz in range(side):
        mapped = mapped + dot(spread[:, zz * span : (zz + 1) * span], wbuf[zz].reshape(span, LANES))
    mapped = mapped.astype(bf16)
    kvbuf[z, y] = mapped[2 * half_rows :].reshape(2, HALF, LANES)
    queries = jnp.concatenate(
        [mapped[n * half_rows : (n + 1) * half_rows, k * DH : (k + 1) * DH] for n in range(2) for k in range(2)],
        axis=0,
    )

    patches = (kvbuf, kv_recv, kv_send)
    begin(*patches, 0)
    begin(*patches, 1)

    query_at = chip * half_rows + lax.rem(iota((1, GQ * half_rows), 1), half_rows)
    key_index = iota((side * HALF, 1), 0)
    top_ref[...] = jnp.full(top_ref.shape, NEG, f32)
    total_ref[...] = jnp.zeros(total_ref.shape, f32)
    mix_ref[...] = jnp.zeros(mix_ref.shape, f32)

    def attend(half, b):
        if half == 0:
            pair_of = kvbuf[:, b, 0]
            key_at = (key_index // HALF * side + b) * half_rows
        else:
            pair_of = kvbuf[b, :, 1]
            key_at = (key_index // HALF + b * side) * half_rows + HALF
        pair_of = pair_of.reshape(side * HALF, LANES)
        logits = dot(pair_of[:, :DH], queries, ((1,), (1,))) / math.sqrt(DH)
        logits = jnp.where(key_at + lax.rem(key_index, HALF) <= query_at, logits, NEG)
        old = top_ref[...]
        new = jnp.maximum(old, jnp.max(logits, axis=0, keepdims=True))
        raised = jnp.exp(logits - new)
        keep = jnp.exp(old - new)
        top_ref[...] = new
        total_ref[...] = total_ref[...] * keep + jnp.sum(raised, axis=0, keepdims=True)
        mix_ref[...] = mix_ref[...] * keep + dot(pair_of[:, DH:], raised.astype(bf16), ((0,), (0,)))

    stage(*patches, 0)
    for distance in range(1, side // 2 + 1):
        stage(*patches, distance)
        for half in (0, 1):
            b0 = own_of(half)[1]
            if distance == 1:
                attend(half, b0)
            else:
                attend(half, wrap(b0 + distance - 1))
                attend(half, wrap(b0 - distance + 1))
    for half in (0, 1):
        attend(half, wrap(own_of(half)[1] + side // 2))

    mixed = (mix_ref[...] / total_ref[...]).T
    mixed = jnp.concatenate([mixed[h * half_rows : (h + 1) * half_rows] for h in range(GQ)], axis=1).astype(bf16)
    own_out = jnp.where(first_core, mixed[:HALF], mixed[HALF:])
    out_send[...] = jnp.where(first_core, mixed[HALF:], mixed[:HALF])
    last = copy(out_send, out_got, out_send_sem, out_recv, sibling)
    last.start()
    for one in to_sibling[:1] + to_sibling[2:] + to_block + to_pair:
        one.wait_send()
    to_sibling[1].wait_send()
    arrived(key_z.at[pl.ds(0, side - 1)], keyz_send)
    arrived(key_y.at[pl.ds(0, side - 1)], keyy_send)
    sent(wbuf, w_send)
    sent(kvbuf, kv_send)
    last.wait()
    theirs = out_got[...]
    out_ref[:, : GQ * DH] = jnp.where(first_core, own_out, theirs)
    out_ref[:, GQ * DH :] = jnp.where(first_core, theirs, own_out)


def on_device(seq, byte_rows, norm_gain, key_weight, value_weight, pool_query, patch_starts):
    side = math.isqrt(seq // 2)
    rows, width = byte_rows.shape
    gathered = (side, side, 2, HALF, LANES)
    dma = pltpu.SemaphoreType.DMA
    scratch = [
        pltpu.VMEM(gathered, bf16),
        pltpu.VMEM(gathered, bf16),
        pltpu.VMEM((HALF, LANES), bf16),
        pltpu.VMEM((rows, width), bf16),
        pltpu.VMEM((2 * rows, width), bf16),
        pltpu.VMEM((4, 1, 128), jnp.int32),
        pltpu.VMEM((1, 1, 128), f32),
        pltpu.VMEM((1, 1, 128), f32),
        pltpu.VMEM((side, 1, 128), f32),
        pltpu.VMEM((side, side, 128), f32),
        pltpu.VMEM((2, 2 * HALF, width), bf16),
        pltpu.VMEM((2, 2 * HALF, width), f32),
        pltpu.VMEM((2 * HALF, width), bf16),
        pltpu.VMEM((8, 128), f32),
        pltpu.VMEM((8, 128), f32),
        pltpu.VMEM((6 * HALF, side * side * 2 * HALF), bf16),
        pltpu.VMEM((1, 2 * HALF * GQ), f32),
        pltpu.VMEM((1, 2 * HALF * GQ), f32),
        pltpu.VMEM((DH, 2 * HALF * GQ), f32),
        pltpu.VMEM((HALF, GQ * DH), bf16),
        pltpu.VMEM((HALF, GQ * DH), bf16),
        dma((side, side, 2)),
        dma((side, side, 2)),
        dma((3,)),
        dma((4,)),
        dma((side,)),
        dma((side,)),
        dma((2,)),
        dma(()),
        dma((2, 2)),
        dma((2, 2)),
        dma((3,)),
        dma((3,)),
        dma(()),
        dma(()),
        dma((2,)),
        dma(()),
    ]
    vmem = pl.BlockSpec(memory_space=pltpu.VMEM)
    return pl.pallas_call(
        functools.partial(kernel, side),
        out_shape=jax.ShapeDtypeStruct((HALF, 2 * GQ * DH), bf16),
        in_specs=[vmem] * 6,
        out_specs=vmem,
        scratch_shapes=scratch,
        compiler_params=pltpu.CompilerParams(
            collective_id=0, has_side_effects=True, vmem_limit_bytes=48 * 1024 * 1024
        ),
    )(
        byte_rows,
        norm_gain.reshape(1, width),
        key_weight,
        value_weight,
        pool_query,
        patch_starts.reshape(1, -1),
    )


def solution(mesh):
    return jax.shard_map(
        functools.partial(on_device, mesh.shape["seq"]),
        mesh=mesh,
        in_specs=(
            P(("dp", "seq"), None),
            P(),
            P("seq", "mp"),
            P("seq", "mp"),
            P("mp", None),
            P(("dp", "seq")),
        ),
        out_specs=P(("dp", "seq"), "mp"),
        check_vma=False,
    )
```

```python
import functools
import math

import jax
import jax.numpy as jnp
from jax import lax
from jax.experimental import pallas as pl
from jax.experimental.pallas import tpu as pltpu
from jax.sharding import PartitionSpec as P

DH = 128
GQ = 4
VW = 768
HALF = 32
LANES = 256
NEG = -1e30
MESH = pl.DeviceIdType.MESH
f32 = jnp.float32
bf16 = jnp.bfloat16


def iota(shape, dim):
    return lax.broadcasted_iota(jnp.int32, shape, dim)


def dot(a, b, dims=((1,), (0,))):
    return lax.dot_general(a, b, (dims, ((), ())), preferred_element_type=f32)


def kernel(
    side,
    bytes_in,
    gain_in,
    kw_in,
    vw_in,
    pq_in,
    starts_in,
    out_ref,
    bytes_ref,
    gain_ref,
    kw_ref,
    vw_ref,
    pq_ref,
    starts_ref,
    wbuf,
    kvbuf,
    wstage,
    sib_bytes,
    normed,
    starts_buf,
    key_stage,
    key_z,
    key_y,
    send_rows,
    own_rows,
    got_rows,
    send_stats,
    got_stats,
    spread,
    pick_ref,
    lane_ref,
    member_ref,
    choose_ref,
    top_ref,
    total_ref,
    mix_ref,
    out_send,
    out_got,
    load_sem,
    w_recv,
    kv_recv,
    sib_recv,
    starts_recv,
    keyz_recv,
    keyy_recv,
    pair_recv,
    out_recv,
    w_send,
    kv_send,
    sib_send,
    starts_send,
    keyz_send,
    keyy_send,
    pair_send,
    out_send_sem,
):
    me = lax.axis_index("seq")
    core = lax.rem(me, 2)
    y = lax.rem(me // 2, side)
    z = me // (2 * side)
    chip = me // 2
    block_at = lax.rem(me, 4)
    pair_at = lax.rem(chip, 2)
    width = bytes_ref.shape[1]
    rows = bytes_ref.shape[0]

    def at(zz, yy, cc):
        return (zz * side + yy) * 2 + cc

    sibling = at(z, y, 1 - core)
    pair_y = y + 1 - 2 * pair_at
    pair = at(z, pair_y, core)
    cross = at(z, pair_y, 1 - core)

    def wrap(index):
        return lax.rem(index + 2 * side, side)

    def copy(src, dst, send_sem, recv_sem, target):
        return pltpu.make_async_remote_copy(
            src_ref=src,
            dst_ref=dst,
            send_sem=send_sem,
            recv_sem=recv_sem,
            device_id={"seq": target},
            device_id_type=MESH,
        )

    def arrived(ref, sem):
        pltpu.make_async_copy(ref, ref, sem).wait()

    loads = [
        pltpu.make_async_copy(src, dst, load_sem.at[k])
        for k, (src, dst) in enumerate(
            (
                (kw_in, kw_ref),
                (pq_in, pq_ref),
                (vw_in, vw_ref),
                (starts_in, starts_ref),
                (bytes_in, bytes_ref),
                (gain_in, gain_ref),
            )
        )
    ]
    for one in loads:
        one.start()

    barrier = pltpu.get_barrier_semaphore()

    def greet(target):
        pl.semaphore_signal(barrier, inc=1, device_id={"seq": target}, device_id_type=MESH)

    @pl.loop(1, side)
    def _(i):
        greet(at(wrap(z + i), y, core))
        greet(at(wrap(z + i), y, 1 - core))
        greet(at(z, wrap(y + i), core))

    greet(sibling)
    greet(cross)

    for one in loads[:2]:
        one.wait()
    folded = kw_ref[...].astype(f32)
    depth = folded.shape[0]
    row_at = iota((depth, 128), 0)
    lane_at = iota((depth, 128), 1)
    for head in range(2):
        col = jnp.sum(folded[:, head * DH : (head + 1) * DH] * pq_ref[head : head + 1, :], axis=1, keepdims=True)
        key_stage[head] = jnp.sum(jnp.where(lane_at == row_at + core * 16, col, 0.0), axis=0, keepdims=True)
    key_z[z * 2 + core] = key_stage[core]

    loads[2].wait()
    part = vw_ref[...].astype(f32)
    first_core = core == 0
    pieces = []
    for head in range(2):
        cuts = [part[:, head * VW + n * LANES : head * VW + (n + 1) * LANES] for n in range(VW // LANES)]
        cuts.append(jnp.zeros((HALF - depth * len(cuts), LANES), f32))
        pieces.append(jnp.concatenate(cuts, axis=0).astype(bf16))
    wbuf[z, y, core] = jnp.where(first_core, pieces[0], pieces[1])
    wstage[...] = jnp.where(first_core, pieces[1], pieces[0])

    loads[3].wait()
    starts_buf[block_at] = jnp.concatenate(
        [starts_ref[...].reshape(1, HALF), jnp.zeros((1, 128 - HALF), jnp.int32)], axis=1
    )

    pl.semaphore_wait(barrier, 3 * side - 1)

    def ref_of(buf, half, a, b):
        return buf.at[a, b, 0] if half == 0 else buf.at[b, a, 1]

    def dev_of(half, a, b):
        return at(a, b, core) if half == 0 else at(b, a, core)

    def own_of(half):
        return (z, y) if half == 0 else (y, z)

    def sem_of(sems, half, a, b):
        return sems.at[a, b, 0] if half == 0 else sems.at[b, a, 1]

    def ring(buf, recv, send, half, a, b, step):
        a0, b0 = own_of(half)
        ref = ref_of(buf, half, a, b)
        copy(
            ref, ref, send.at[half, 1], sem_of(recv, half, a, b), dev_of(half, a0, wrap(b0 + step))
        ).start()

    def pass_on(buf, recv, send, half, a, b, step, distance, even):
        last = distance == side // 2 - 1
        if not last or even == (step == 1):
            ring(buf, recv, send, half, a, b, step)

    def begin(buf, recv, send, half):
        a0, b0 = own_of(half)
        ref = ref_of(buf, half, a0, b0)
        for step in (1, -1):
            pass_on(buf, recv, send, half, a0, b0, step, 0, True)

        @pl.loop(1, side)
        def _(i):
            copy(
                ref, ref, send.at[half, 0], sem_of(recv, half, a0, b0), dev_of(half, wrap(a0 + i), b0)
            ).start()

    def visit(buf, recv, send, distance, t):
        for half in (0, 1):
            a0, b0 = own_of(half)
            for even, a in ((True, wrap(a0 - t)), (False, wrap(a0 + t + 1))):
                if distance == 0:

                    def take(half=half, a=a, b0=b0, even=even):
                        arrived(ref_of(buf, half, a, b0), sem_of(recv, half, a, b0))
                        for step in (1, -1):
                            pass_on(buf, recv, send, half, a, b0, step, 0, even)

                    if even:
                        pl.when(t > 0)(take)
                    else:
                        take()
                elif distance < side // 2:
                    for step in (1, -1):
                        b = wrap(b0 - step * distance)
                        arrived(ref_of(buf, half, a, b), sem_of(recv, half, a, b))
                        pass_on(buf, recv, send, half, a, b, step, distance, even)
                else:
                    b = wrap(b0 + distance)
                    arrived(ref_of(buf, half, a, b), sem_of(recv, half, a, b))

    def stage(buf, recv, send, distance):
        @pl.loop(0, side // 2)
        def _(t):
            visit(buf, recv, send, distance, t)

    def sent(buf, send):
        for half in (0, 1):
            ref = buf.at[0, pl.ds(0, side - 1), half]
            arrived(ref, send.at[half, 0])
            ref = buf.at[:, pl.ds(0, side - 1), half]
            arrived(ref, send.at[half, 1])

    weights = (wbuf, w_recv, w_send)
    sib_piece = wbuf.at[z, y, 1 - core]
    chips = side * side
    half_rows = 2 * HALF
    window = min(256, width)
    blocks = side * side * 2 * HALF // 128
    lefts = [min(4 * depth * b // 128 * 128, width - window) for b in range(blocks)]

    def send_keys():
        def keys_to(target, head):
            copy(key_stage.at[head], key_z.at[z * 2 + core], keyz_send, keyz_recv, target).start()

        @pl.loop(1, side)
        def _(i):
            for head in range(2):
                keys_to(at(wrap(z + i), y, head), head)

        keys_to(sibling, 1 - core)

    def send_piece():
        to_sibling[0].start()

    def send_bytes():
        loads[4].wait()
        to_sibling[1].start()

    def send_starts():
        for one in to_block:
            one.start()

    def begin_weights():
        @pl.when(first_core)
        def _():
            begin(*weights, 0)
            arrived(sib_piece, sib_recv.at[0])
            begin(*weights, 1)

        @pl.when(core == 1)
        def _():
            begin(*weights, 1)
            arrived(sib_piece, sib_recv.at[0])
            begin(*weights, 0)

    def norm_rows(ref, first, quarter):
        @pl.loop(quarter * rows // 128, (quarter + 1) * rows // 128)
        def _(i):
            at_row = pl.multiple_of(i * 32, 32)
            wide = ref[pl.ds(at_row, 32), :].astype(f32)
            scale = lax.rsqrt(jnp.mean(wide * wide, axis=-1, keepdims=True) + 1e-05)
            normed[pl.ds(pl.multiple_of(first + at_row, 32), 32), :] = (
                wide * scale * gain_ref[...].reshape(1, width)
            ).astype(bf16)

    def norm_own(quarter):
        if quarter == 0:
            loads[5].wait()
        norm_rows(bytes_ref, core * rows, quarter)

    def norm_sibling(quarter):
        if quarter == 0:
            arrived(sib_bytes, sib_recv.at[1])
        norm_rows(sib_bytes, (1 - core) * rows, quarter)

    def pass_keys():
        arrived(key_z.at[pl.ds(0, 2 * side - 1)], keyz_recv)
        key_y[y] = jnp.concatenate([key_z[2 * i] + key_z[2 * i + 1] for i in range(side)], axis=0)

        @pl.loop(1, side)
        def _(i):
            copy(key_y.at[y], key_y.at[y], keyy_send, keyy_recv, at(z, wrap(y + i), core)).start()

    def make_pick():
        column = iota((1, width), 1)
        column_chip = column // (2 * depth)
        column_row = lax.rem(column_chip, side) * side + column_chip // side
        pick_ref[...] = jnp.where(iota((chips, width), 0) == column_row, 1.0, 0.0).astype(bf16)
        column_lane = lax.rem(column // depth, 2) * 16 + lax.rem(column, depth)
        lane_row = iota((128, width), 0)
        lane_ref[...] = jnp.where(lax.rem(lane_row, 32) == column_lane, 1.0, 0.0)

    def make_member():
        for k in range(1, 4):
            other = lax.rem(block_at + k, 4)
            arrived(starts_buf.at[other], starts_recv.at[other])
        patch_sub = iota((HALF, 128), 0)
        patch_lane = iota((HALF, 128), 1)
        first_cols, next_cols = [], []
        for q in range(4):
            row = starts_buf[q]
            follow = (chip // 2 + 1) * (4 * rows) if q == 3 else starts_buf[q + 1][:, 0:1]
            row = jnp.where(iota((1, 128), 1) == HALF, follow, row)
            first_cols.append(jnp.sum(jnp.where(patch_lane == patch_sub, row, 0), axis=1, keepdims=True))
            next_cols.append(jnp.sum(jnp.where(patch_lane == patch_sub + 1, row, 0), axis=1, keepdims=True))
        first_col = jnp.concatenate(first_cols, axis=0)
        next_col = jnp.concatenate(next_cols, axis=0)
        position = chip * (2 * rows) + iota((1, 2 * rows), 1)
        member_ref[...] = jnp.where((first_col <= position) & (position < next_col), 1.0, 0.0)

    def make_choose():
        lane = iota((1, 128), 1)
        in_piece = lax.rem(lane, HALF)
        source = jnp.where(in_piece < 3 * depth, (lane // HALF) * depth + lax.rem(in_piece, depth), -100000)
        sub = iota((window, 128), 0)
        for b in range(blocks):
            choose_ref[b] = jnp.where(sub == source + (4 * depth * b - lefts[b]), 1.0, 0.0).astype(bf16)

    def pool():
        arrived(key_y.at[pl.ds(0, side - 1)], keyy_recv)
        table = key_y[...].reshape(chips, 128)
        high = table.astype(bf16).astype(f32)
        middle = (table - high).astype(bf16).astype(f32)
        low = (table - high - middle).astype(bf16).astype(f32)
        packed = (high + pltpu.roll(middle, 32, axis=1) + pltpu.roll(low, 64, axis=1)).astype(bf16)
        taken = dot(packed, pick_ref[...], ((0,), (0,)))
        key_rows = (taken * lane_ref[...]).astype(bf16)
        scores = jnp.sum(dot(key_rows, normed[...], ((1,), (1,))), axis=0, keepdims=True) / math.sqrt(DH)
        member = member_ref[...] > 0.5
        masked = jnp.where(member, scores, NEG)
        top = jnp.max(masked, axis=1, keepdims=True)
        weight = jnp.where(member, jnp.exp(masked - top), 0.0).astype(bf16)
        total = jnp.sum(weight.astype(f32), axis=1, keepdims=True)
        share = jnp.where(total > 0.0, 1.0 / jnp.maximum(total, 1e-30), 0.0)
        pooled_rows = dot(weight, normed[...]) * share
        own_rows[...] = pooled_rows.reshape(2, half_rows, width)
        send_rows[...] = pooled_rows.astype(bf16).reshape(2, half_rows, width)
        to_pair[0].start()
        eye = iota((4 * HALF, 128), 0) == iota((4 * HALF, 128), 1)
        top_row = jnp.sum(jnp.where(eye, top, 0.0), axis=0, keepdims=True)
        total_row = jnp.sum(jnp.where(eye, total, 0.0), axis=0, keepdims=True)
        send_stats[...] = jnp.concatenate([top_row, total_row, jnp.zeros((6, 128), f32)], axis=0)
        to_pair[1].start()

    def merge():
        to_pair[1].wait_recv()
        eye = iota((half_rows, 128), 1) == iota((half_rows, 128), 0) + pair_at * half_rows

        def to_column(row):
            return jnp.sum(jnp.where(eye, row, 0.0), axis=1, keepdims=True)

        own_top, own_total = to_column(send_stats[0:1, :]), to_column(send_stats[1:2, :])
        got_top, got_total = to_column(got_stats[0:1, :]), to_column(got_stats[1:2, :])
        top = jnp.maximum(own_top, got_top)
        own_part = jnp.exp(own_top - top) * own_total
        got_part = jnp.exp(got_top - top) * got_total
        share = 1.0 / (own_part + got_part)
        to_pair[0].wait_recv()
        merged = own_rows[pair_at] * (own_part * share) + got_rows[...].astype(f32) * (got_part * share)
        merged = merged.astype(bf16)
        which = lax.rem(iota((1, 128), 1), HALF) // depth
        for b in range(blocks):
            block = dot(merged[:, lefts[b] : lefts[b] + window], choose_ref[b])
            for n in range(3):
                spread[n * half_rows : (n + 1) * half_rows, b * 128 : (b + 1) * 128] = jnp.where(
                    which == n, block, 0.0
                ).astype(bf16)

    to_sibling = [
        copy(wstage, wbuf.at[z, y, core], sib_send.at[0], sib_recv.at[0], sibling),
        copy(bytes_ref, sib_bytes, sib_send.at[1], sib_recv.at[1], sibling),
    ]
    to_block = [
        copy(starts_buf.at[block_at], starts_buf.at[block_at], starts_send.at[k], starts_recv.at[block_at], target)
        for k, target in enumerate((sibling, pair, cross))
    ]
    to_pair = [
        copy(send_rows.at[1 - pair_at], got_rows, pair_send.at[0], pair_recv.at[0], pair),
        copy(send_stats, got_stats, pair_send.at[1], pair_recv.at[1], pair),
    ]
    send_keys()
    send_piece()
    send_starts()
    send_bytes()
    begin_weights()
    norm_own(0)
    norm_own(1)
    norm_own(2)
    norm_own(3)
    pass_keys()
    stage(*weights, 0)
    norm_sibling(0)
    norm_sibling(1)
    norm_sibling(2)
    norm_sibling(3)
    stage(*weights, 1)
    make_pick()
    make_member()
    stage(*weights, 2)
    pool()
    stage(*weights, 3)
    make_choose()
    stage(*weights, 4)
    merge()
    span = side * 2 * HALF

    def mapped(low, high):
        total = jnp.zeros(((high - low) * half_rows, LANES), f32)
        for zz in range(side):
            total = total + dot(
                spread[low * half_rows : high * half_rows, zz * span : (zz + 1) * span],
                wbuf[zz].reshape(span, LANES),
            )
        return total.astype(bf16)

    patches = (kvbuf, kv_recv, kv_send)
    kvbuf[z, y] = mapped(2, 3).reshape(2, HALF, LANES)
    begin(*patches, 0)
    begin(*patches, 1)
    mapped_queries = mapped(0, 2)
    queries = jnp.concatenate(
        [mapped_queries[n * half_rows : (n + 1) * half_rows, k * DH : (k + 1) * DH] for n in range(2) for k in range(2)],
        axis=0,
    )

    query_at = chip * half_rows + lax.rem(iota((1, GQ * half_rows), 1), half_rows)
    key_index = iota((side * HALF, 1), 0)
    top_ref[...] = jnp.full(top_ref.shape, NEG, f32)
    total_ref[...] = jnp.zeros(total_ref.shape, f32)
    mix_ref[...] = jnp.zeros(mix_ref.shape, f32)

    def attend(half, b):
        if half == 0:
            pair_of = kvbuf[:, b, 0]
            key_at = (key_index // HALF * side + b) * half_rows
        else:
            pair_of = kvbuf[b, :, 1]
            key_at = (key_index // HALF + b * side) * half_rows + HALF
        pair_of = pair_of.reshape(side * HALF, LANES)
        logits = dot(pair_of[:, :DH], queries, ((1,), (1,))) / math.sqrt(DH)
        logits = jnp.where(key_at + lax.rem(key_index, HALF) <= query_at, logits, NEG)
        old = top_ref[...]
        new = jnp.maximum(old, jnp.max(logits, axis=0, keepdims=True))
        raised = jnp.exp(logits - new)
        keep = jnp.exp(old - new)
        top_ref[...] = new
        total_ref[...] = total_ref[...] * keep + jnp.sum(raised, axis=0, keepdims=True)
        mix_ref[...] = mix_ref[...] * keep + dot(pair_of[:, DH:], raised.astype(bf16), ((0,), (0,)))

    def ready_at(distance):
        for half in (0, 1):
            b0 = own_of(half)[1]
            if distance == 0:
                yield half, b0
            elif distance == side // 2:
                yield half, wrap(b0 + distance)
            else:
                yield half, wrap(b0 + distance)
                yield half, wrap(b0 - distance)

    queue = []
    for distance in range(side // 2 + 1):
        for t in range(side // 2):
            visit(*patches, distance, t)
            if queue:
                attend(*queue.pop(0))
        queue += list(ready_at(distance))
    for one in queue:
        attend(*one)

    mixed = (mix_ref[...] / total_ref[...]).T
    mixed = jnp.concatenate([mixed[h * half_rows : (h + 1) * half_rows] for h in range(GQ)], axis=1).astype(bf16)
    own_out = jnp.where(first_core, mixed[:HALF], mixed[HALF:])
    out_send[...] = jnp.where(first_core, mixed[HALF:], mixed[:HALF])
    last = copy(out_send, out_got, out_send_sem, out_recv, sibling)
    last.start()
    for one in to_sibling + to_block + to_pair:
        one.wait_send()
    arrived(key_z.at[pl.ds(0, 2 * side - 1)], keyz_send)
    arrived(key_y.at[pl.ds(0, side - 1)], keyy_send)
    sent(wbuf, w_send)
    sent(kvbuf, kv_send)
    last.wait()
    theirs = out_got[...]
    out_ref[:, : GQ * DH] = jnp.where(first_core, own_out, theirs)
    out_ref[:, GQ * DH :] = jnp.where(first_core, theirs, own_out)


def on_device(seq, byte_rows, norm_gain, key_weight, value_weight, pool_query, patch_starts):
    side = math.isqrt(seq // 2)
    rows, width = byte_rows.shape
    gathered = (side, side, 2, HALF, LANES)
    dma = pltpu.SemaphoreType.DMA
    scratch = [
        pltpu.VMEM((rows, width), bf16),
        pltpu.VMEM(norm_gain.shape, f32),
        pltpu.VMEM(key_weight.shape, bf16),
        pltpu.VMEM(value_weight.shape, bf16),
        pltpu.VMEM(pool_query.shape, f32),
        pltpu.VMEM(patch_starts.shape, jnp.int32),
        pltpu.VMEM(gathered, bf16),
        pltpu.VMEM(gathered, bf16),
        pltpu.VMEM((HALF, LANES), bf16),
        pltpu.VMEM((rows, width), bf16),
        pltpu.VMEM((2 * rows, width), bf16),
        pltpu.VMEM((4, 1, 128), jnp.int32),
        pltpu.VMEM((2, 1, 128), f32),
        pltpu.VMEM((2 * side, 1, 128), f32),
        pltpu.VMEM((side, side, 128), f32),
        pltpu.VMEM((2, 2 * HALF, width), bf16),
        pltpu.VMEM((2, 2 * HALF, width), f32),
        pltpu.VMEM((2 * HALF, width), bf16),
        pltpu.VMEM((8, 128), f32),
        pltpu.VMEM((8, 128), f32),
        pltpu.VMEM((6 * HALF, side * side * 2 * HALF), bf16),
        pltpu.VMEM((side * side, width), bf16),
        pltpu.VMEM((128, width), f32),
        pltpu.VMEM((4 * HALF, 2 * rows), f32),
        pltpu.VMEM((side * side * 2 * HALF // 128, min(256, width), 128), bf16),
        pltpu.VMEM((1, 2 * HALF * GQ), f32),
        pltpu.VMEM((1, 2 * HALF * GQ), f32),
        pltpu.VMEM((DH, 2 * HALF * GQ), f32),
        pltpu.VMEM((HALF, GQ * DH), bf16),
        pltpu.VMEM((HALF, GQ * DH), bf16),
        dma((6,)),
        dma((side, side, 2)),
        dma((side, side, 2)),
        dma((2,)),
        dma((4,)),
        dma(()),
        dma(()),
        dma((2,)),
        dma(()),
        dma((2, 2)),
        dma((2, 2)),
        dma((2,)),
        dma((3,)),
        dma(()),
        dma(()),
        dma((2,)),
        dma(()),
    ]
    return pl.pallas_call(
        functools.partial(kernel, side),
        out_shape=jax.ShapeDtypeStruct((HALF, 2 * GQ * DH), bf16),
        in_specs=[pl.BlockSpec(memory_space=pl.ANY)] * 6,
        out_specs=pl.BlockSpec(memory_space=pltpu.VMEM),
        scratch_shapes=scratch,
        compiler_params=pltpu.CompilerParams(
            collective_id=0, has_side_effects=True, vmem_limit_bytes=60 * 1024 * 1024
        ),
    )(byte_rows, norm_gain, key_weight, value_weight, pool_query, patch_starts)


def solution(mesh):
    return jax.shard_map(
        functools.partial(on_device, mesh.shape["seq"]),
        mesh=mesh,
        in_specs=(
            P(("dp", "seq"), None),
            P(),
            P("seq", "mp"),
            P("seq", "mp"),
            P("mp", None),
            P(("dp", "seq")),
        ),
        out_specs=P(("dp", "seq"), "mp"),
        check_vma=False,
    )
```

```python
import functools
import math

import jax
import jax.numpy as jnp
from jax import lax
from jax.experimental import pallas as pl
from jax.experimental.pallas import tpu as pltpu
from jax.sharding import PartitionSpec as P

DH = 128
GQ = 4
VW = 768
HALF = 32
LANES = 256
NEG = -1e30
MESH = pl.DeviceIdType.MESH
f32 = jnp.float32
bf16 = jnp.bfloat16


def iota(shape, dim):
    return lax.broadcasted_iota(jnp.int32, shape, dim)


def dot(a, b, dims=((1,), (0,))):
    return lax.dot_general(a, b, (dims, ((), ())), preferred_element_type=f32)


def kernel(
    side,
    bytes_in,
    gain_in,
    kw_in,
    vw_in,
    pq_in,
    starts_in,
    out_ref,
    bytes_ref,
    gain_ref,
    kw_ref,
    vw_ref,
    pq_ref,
    starts_ref,
    wbuf,
    kvbuf,
    wstage,
    sib_bytes,
    normed,
    starts_buf,
    key_stage,
    key_z,
    key_y,
    send_rows,
    own_rows,
    got_rows,
    send_stats,
    got_stats,
    spread,
    pick_ref,
    lane_ref,
    member_ref,
    choose_ref,
    score_ref,
    top_ref,
    total_ref,
    mix_ref,
    out_send,
    out_got,
    load_sem,
    w_recv,
    kv_recv,
    sib_recv,
    starts_recv,
    keyz_recv,
    keyy_recv,
    pair_recv,
    out_recv,
    w_send,
    kv_send,
    sib_send,
    starts_send,
    keyz_send,
    keyy_send,
    pair_send,
    out_send_sem,
):
    me = lax.axis_index("seq")
    core = lax.rem(me, 2)
    y = lax.rem(me // 2, side)
    z = me // (2 * side)
    chip = me // 2
    block_at = lax.rem(me, 4)
    pair_at = lax.rem(chip, 2)
    width = bytes_ref.shape[1]
    rows = bytes_ref.shape[0]

    def at(zz, yy, cc):
        return (zz * side + yy) * 2 + cc

    sibling = at(z, y, 1 - core)
    pair_y = y + 1 - 2 * pair_at
    pair = at(z, pair_y, core)
    cross = at(z, pair_y, 1 - core)

    def wrap(index):
        return lax.rem(index + 2 * side, side)

    def copy(src, dst, send_sem, recv_sem, target):
        return pltpu.make_async_remote_copy(
            src_ref=src,
            dst_ref=dst,
            send_sem=send_sem,
            recv_sem=recv_sem,
            device_id={"seq": target},
            device_id_type=MESH,
        )

    def arrived(ref, sem):
        pltpu.make_async_copy(ref, ref, sem).wait()

    loads = [
        pltpu.make_async_copy(src, dst, load_sem.at[k])
        for k, (src, dst) in enumerate(
            (
                (kw_in, kw_ref),
                (pq_in, pq_ref),
                (vw_in, vw_ref),
                (starts_in, starts_ref),
                (bytes_in, bytes_ref),
                (gain_in, gain_ref),
            )
        )
    ]
    for one in loads:
        one.start()

    barrier = pltpu.get_barrier_semaphore()

    def greet(target):
        pl.semaphore_signal(barrier, inc=1, device_id={"seq": target}, device_id_type=MESH)

    @pl.loop(1, side)
    def _(i):
        greet(at(wrap(z + i), y, core))
        greet(at(wrap(z + i), y, 1 - core))
        greet(at(z, wrap(y + i), core))

    greet(sibling)
    greet(cross)

    for one in loads[:2]:
        one.wait()
    folded = kw_ref[...].astype(f32)
    depth = folded.shape[0]
    row_at = iota((depth, 128), 0)
    lane_at = iota((depth, 128), 1)
    for head in range(2):
        col = jnp.sum(folded[:, head * DH : (head + 1) * DH] * pq_ref[head : head + 1, :], axis=1, keepdims=True)
        key_stage[head] = jnp.sum(jnp.where(lane_at == row_at + core * 16, col, 0.0), axis=0, keepdims=True)
    key_z[z * 2 + core] = key_stage[core]

    loads[2].wait()
    part = vw_ref[...].astype(f32)
    first_core = core == 0
    pieces = []
    for head in range(2):
        cuts = [part[:, head * VW + n * LANES : head * VW + (n + 1) * LANES] for n in range(VW // LANES)]
        cuts.append(jnp.zeros((HALF - depth * len(cuts), LANES), f32))
        pieces.append(jnp.concatenate(cuts, axis=0).astype(bf16))
    wbuf[z, y, core] = jnp.where(first_core, pieces[0], pieces[1])
    wstage[...] = jnp.where(first_core, pieces[1], pieces[0])

    loads[3].wait()
    starts_buf[block_at] = jnp.concatenate(
        [starts_ref[...].reshape(1, HALF), jnp.zeros((1, 128 - HALF), jnp.int32)], axis=1
    )

    pl.semaphore_wait(barrier, 3 * side - 1)

    def ref_of(buf, half, a, b):
        return buf.at[a, b, 0] if half == 0 else buf.at[b, a, 1]

    def dev_of(half, a, b):
        return at(a, b, core) if half == 0 else at(b, a, core)

    def own_of(half):
        return (z, y) if half == 0 else (y, z)

    def sem_of(sems, half, a, b):
        return sems.at[a, b, 0] if half == 0 else sems.at[b, a, 1]

    def ring(buf, recv, send, half, a, b, step):
        a0, b0 = own_of(half)
        ref = ref_of(buf, half, a, b)
        copy(
            ref, ref, send.at[half, 1], sem_of(recv, half, a, b), dev_of(half, a0, wrap(b0 + step))
        ).start()

    def pass_on(buf, recv, send, half, a, b, step, distance, even):
        last = distance == side // 2 - 1
        if not last or even == (step == 1):
            ring(buf, recv, send, half, a, b, step)

    def begin(buf, recv, send, half):
        a0, b0 = own_of(half)
        ref = ref_of(buf, half, a0, b0)
        for step in (1, -1):
            pass_on(buf, recv, send, half, a0, b0, step, 0, True)

        @pl.loop(1, side)
        def _(i):
            copy(
                ref, ref, send.at[half, 0], sem_of(recv, half, a0, b0), dev_of(half, wrap(a0 + i), b0)
            ).start()

    def visit(buf, recv, send, distance, t, halves=(0, 1)):
        for half in halves:
            a0, b0 = own_of(half)
            for even, a in ((True, wrap(a0 - t)), (False, wrap(a0 + t + 1))):
                if distance == 0:

                    def take(half=half, a=a, b0=b0, even=even):
                        arrived(ref_of(buf, half, a, b0), sem_of(recv, half, a, b0))
                        for step in (1, -1):
                            pass_on(buf, recv, send, half, a, b0, step, 0, even)

                    if even:
                        pl.when(t > 0)(take)
                    else:
                        take()
                elif distance < side // 2:
                    for step in (1, -1):
                        b = wrap(b0 - step * distance)
                        arrived(ref_of(buf, half, a, b), sem_of(recv, half, a, b))
                        pass_on(buf, recv, send, half, a, b, step, distance, even)
                else:
                    b = wrap(b0 + distance)
                    arrived(ref_of(buf, half, a, b), sem_of(recv, half, a, b))

    def stage(buf, recv, send, distance):
        @pl.loop(0, side // 2)
        def _(t):
            visit(buf, recv, send, distance, t)

    def sent(buf, send):
        for half in (0, 1):
            ref = buf.at[0, pl.ds(0, side - 1), half]
            arrived(ref, send.at[half, 0])
            ref = buf.at[:, pl.ds(0, side - 1), half]
            arrived(ref, send.at[half, 1])

    weights = (wbuf, w_recv, w_send)
    sib_piece = wbuf.at[z, y, 1 - core]
    chips = side * side
    half_rows = 2 * HALF
    window = min(256, width)
    blocks = side * side * 2 * HALF // 128
    lefts = [min(4 * depth * b // 128 * 128, width - window) for b in range(blocks)]

    def send_keys():
        def keys_to(target, head):
            copy(key_stage.at[head], key_z.at[z * 2 + core], keyz_send, keyz_recv, target).start()

        @pl.loop(1, side)
        def _(i):
            for head in range(2):
                keys_to(at(wrap(z + i), y, head), head)

        keys_to(sibling, 1 - core)

    def send_piece():
        to_sibling[0].start()

    def send_bytes():
        loads[4].wait()
        to_sibling[1].start()

    def send_starts():
        for one in to_block:
            one.start()

    def begin_weights():
        @pl.when(first_core)
        def _():
            begin(*weights, 0)
            arrived(sib_piece, sib_recv.at[0])
            begin(*weights, 1)

        @pl.when(core == 1)
        def _():
            begin(*weights, 1)
            arrived(sib_piece, sib_recv.at[0])
            begin(*weights, 0)

    def norm_rows(ref, first, quarter):
        @pl.loop(quarter * rows // 128, (quarter + 1) * rows // 128)
        def _(i):
            at_row = pl.multiple_of(i * 32, 32)
            wide = ref[pl.ds(at_row, 32), :].astype(f32)
            scale = lax.rsqrt(jnp.mean(wide * wide, axis=-1, keepdims=True) + 1e-05)
            normed[pl.ds(pl.multiple_of(first + at_row, 32), 32), :] = (
                wide * scale * gain_ref[...].reshape(1, width)
            ).astype(bf16)

    def norm_own(quarter):
        if quarter == 0:
            loads[5].wait()
        norm_rows(bytes_ref, core * rows, quarter)

    def norm_sibling(quarter):
        if quarter == 0:
            arrived(sib_bytes, sib_recv.at[1])
        norm_rows(sib_bytes, (1 - core) * rows, quarter)

    def pass_keys():
        arrived(key_z.at[pl.ds(0, 2 * side - 1)], keyz_recv)
        key_y[y] = jnp.concatenate([key_z[2 * i] + key_z[2 * i + 1] for i in range(side)], axis=0)

        @pl.loop(1, side)
        def _(i):
            copy(key_y.at[y], key_y.at[y], keyy_send, keyy_recv, at(z, wrap(y + i), core)).start()

    def make_pick():
        column = iota((1, width), 1)
        column_chip = column // (2 * depth)
        column_row = lax.rem(column_chip, side) * side + column_chip // side
        pick_ref[...] = jnp.where(iota((chips, width), 0) == column_row, 1.0, 0.0).astype(bf16)
        column_lane = lax.rem(column // depth, 2) * 16 + lax.rem(column, depth)
        lane_row = iota((128, width), 0)
        lane_ref[...] = jnp.where(lax.rem(lane_row, 32) == column_lane, 1.0, 0.0)

    def make_member():
        for k in range(1, 4):
            other = lax.rem(block_at + k, 4)
            arrived(starts_buf.at[other], starts_recv.at[other])
        patch_sub = iota((HALF, 128), 0)
        patch_lane = iota((HALF, 128), 1)
        first_cols, next_cols = [], []
        for q in range(4):
            row = starts_buf[q]
            follow = (chip // 2 + 1) * (4 * rows) if q == 3 else starts_buf[q + 1][:, 0:1]
            row = jnp.where(iota((1, 128), 1) == HALF, follow, row)
            first_cols.append(jnp.sum(jnp.where(patch_lane == patch_sub, row, 0), axis=1, keepdims=True))
            next_cols.append(jnp.sum(jnp.where(patch_lane == patch_sub + 1, row, 0), axis=1, keepdims=True))
        first_col = jnp.concatenate(first_cols, axis=0)
        next_col = jnp.concatenate(next_cols, axis=0)
        position = chip * (2 * rows) + iota((1, 2 * rows), 1)
        member_ref[...] = jnp.where((first_col <= position) & (position < next_col), 1.0, 0.0)

    def make_choose():
        lane = iota((1, 128), 1)
        in_piece = lax.rem(lane, HALF)
        source = jnp.where(in_piece < 3 * depth, (lane // HALF) * depth + lax.rem(in_piece, depth), -100000)
        sub = iota((window, 128), 0)
        for b in range(blocks):
            choose_ref[b] = jnp.where(sub == source + (4 * depth * b - lefts[b]), 1.0, 0.0).astype(bf16)

    def score():
        arrived(key_y.at[pl.ds(0, side - 1)], keyy_recv)
        table = key_y[...].reshape(chips, 128)
        high = table.astype(bf16).astype(f32)
        middle = (table - high).astype(bf16).astype(f32)
        low = (table - high - middle).astype(bf16).astype(f32)
        packed = (high + pltpu.roll(middle, 32, axis=1) + pltpu.roll(low, 64, axis=1)).astype(bf16)
        taken = dot(packed, pick_ref[...], ((0,), (0,)))
        key_rows = (taken * lane_ref[...]).astype(bf16)
        score_ref[...] = jnp.sum(dot(key_rows, normed[...], ((1,), (1,))), axis=0, keepdims=True) / math.sqrt(DH)

    def pool():
        member = member_ref[...] > 0.5
        masked = jnp.where(member, score_ref[...], NEG)
        top = jnp.max(masked, axis=1, keepdims=True)
        weight = jnp.where(member, jnp.exp(masked - top), 0.0).astype(bf16)
        total = jnp.sum(weight.astype(f32), axis=1, keepdims=True)
        share = jnp.where(total > 0.0, 1.0 / jnp.maximum(total, 1e-30), 0.0)
        pooled_rows = dot(weight, normed[...]) * share
        own_rows[...] = pooled_rows.reshape(2, half_rows, width)
        send_rows[...] = pooled_rows.astype(bf16).reshape(2, half_rows, width)
        to_pair[0].start()
        eye = iota((4 * HALF, 128), 0) == iota((4 * HALF, 128), 1)
        top_row = jnp.sum(jnp.where(eye, top, 0.0), axis=0, keepdims=True)
        total_row = jnp.sum(jnp.where(eye, total, 0.0), axis=0, keepdims=True)
        send_stats[...] = jnp.concatenate([top_row, total_row, jnp.zeros((6, 128), f32)], axis=0)
        to_pair[1].start()

    def merge():
        to_pair[1].wait_recv()
        eye = iota((half_rows, 128), 1) == iota((half_rows, 128), 0) + pair_at * half_rows

        def to_column(row):
            return jnp.sum(jnp.where(eye, row, 0.0), axis=1, keepdims=True)

        own_top, own_total = to_column(send_stats[0:1, :]), to_column(send_stats[1:2, :])
        got_top, got_total = to_column(got_stats[0:1, :]), to_column(got_stats[1:2, :])
        top = jnp.maximum(own_top, got_top)
        own_part = jnp.exp(own_top - top) * own_total
        got_part = jnp.exp(got_top - top) * got_total
        share = 1.0 / (own_part + got_part)
        to_pair[0].wait_recv()
        merged = own_rows[pair_at] * (own_part * share) + got_rows[...].astype(f32) * (got_part * share)
        merged = merged.astype(bf16)
        which = lax.rem(iota((1, 128), 1), HALF) // depth
        for b in range(blocks):
            block = dot(merged[:, lefts[b] : lefts[b] + window], choose_ref[b])
            for n in range(3):
                spread[n * half_rows : (n + 1) * half_rows, b * 128 : (b + 1) * 128] = jnp.where(
                    which == n, block, 0.0
                ).astype(bf16)

    to_sibling = [
        copy(wstage, wbuf.at[z, y, core], sib_send.at[0], sib_recv.at[0], sibling),
        copy(bytes_ref, sib_bytes, sib_send.at[1], sib_recv.at[1], sibling),
    ]
    to_block = [
        copy(starts_buf.at[block_at], starts_buf.at[block_at], starts_send.at[k], starts_recv.at[block_at], target)
        for k, target in enumerate((sibling, pair, cross))
    ]
    to_pair = [
        copy(send_rows.at[1 - pair_at], got_rows, pair_send.at[0], pair_recv.at[0], pair),
        copy(send_stats, got_stats, pair_send.at[1], pair_recv.at[1], pair),
    ]
    send_keys()
    send_piece()
    send_starts()
    send_bytes()
    begin_weights()
    norm_own(0)
    norm_own(1)
    norm_own(2)
    norm_own(3)
    pass_keys()
    stage(*weights, 0)
    norm_sibling(0)
    norm_sibling(1)
    norm_sibling(2)
    norm_sibling(3)
    stage(*weights, 1)
    make_pick()
    make_member()
    visit(*weights, 2, 0)
    visit(*weights, 2, 1)
    score()
    visit(*weights, 2, 2)
    visit(*weights, 2, 3)
    pool()
    stage(*weights, 3)
    make_choose()
    merge()
    stage(*weights, 4)
    span = side * 2 * HALF

    def mapped(low, high):
        total = jnp.zeros(((high - low) * half_rows, LANES), f32)
        for zz in range(side):
            total = total + dot(
                spread[low * half_rows : high * half_rows, zz * span : (zz + 1) * span],
                wbuf[zz].reshape(span, LANES),
            )
        return total.astype(bf16)

    patches = (kvbuf, kv_recv, kv_send)
    kvbuf[z, y] = mapped(2, 3).reshape(2, HALF, LANES)
    begin(*patches, 0)
    begin(*patches, 1)
    mapped_queries = mapped(0, 2)
    queries = jnp.concatenate(
        [mapped_queries[n * half_rows : (n + 1) * half_rows, k * DH : (k + 1) * DH] for n in range(2) for k in range(2)],
        axis=0,
    )

    query_at = chip * half_rows + lax.rem(iota((1, GQ * half_rows), 1), half_rows)
    key_index = iota((side * HALF, 1), 0)
    top_ref[...] = jnp.full(top_ref.shape, NEG, f32)
    total_ref[...] = jnp.zeros(total_ref.shape, f32)
    mix_ref[...] = jnp.zeros(mix_ref.shape, f32)

    def attend(half, b):
        if half == 0:
            pair_of = kvbuf[:, b, 0]
            key_at = (key_index // HALF * side + b) * half_rows
        else:
            pair_of = kvbuf[b, :, 1]
            key_at = (key_index // HALF + b * side) * half_rows + HALF
        pair_of = pair_of.reshape(side * HALF, LANES)
        logits = dot(pair_of[:, :DH], queries, ((1,), (1,))) / math.sqrt(DH)
        logits = jnp.where(key_at + lax.rem(key_index, HALF) <= query_at, logits, NEG)
        old = top_ref[...]
        new = jnp.maximum(old, jnp.max(logits, axis=0, keepdims=True))
        raised = jnp.exp(logits - new)
        keep = jnp.exp(old - new)
        top_ref[...] = new
        total_ref[...] = total_ref[...] * keep + jnp.sum(raised, axis=0, keepdims=True)
        mix_ref[...] = mix_ref[...] * keep + dot(pair_of[:, DH:], raised.astype(bf16), ((0,), (0,)))

    def ready_at(distance):
        for half in (0, 1):
            b0 = own_of(half)[1]
            if distance == 0:
                yield half, b0
            else:
                yield half, wrap(b0 + distance)
                yield half, wrap(b0 - distance)

    queue = []
    for distance in range(side // 2):
        for t in range(side // 2):
            visit(*patches, distance, t)
            if queue:
                attend(*queue.pop(0))
        queue += list(ready_at(distance))
    for half in (0, 1):
        for t in range(side // 2):
            visit(*patches, side // 2, t, (half,))
            if queue:
                attend(*queue.pop(0))
        attend(half, wrap(own_of(half)[1] + side // 2))

    mixed = (mix_ref[...] / total_ref[...]).T
    mixed = jnp.concatenate([mixed[h * half_rows : (h + 1) * half_rows] for h in range(GQ)], axis=1).astype(bf16)
    own_out = jnp.where(first_core, mixed[:HALF], mixed[HALF:])
    out_send[...] = jnp.where(first_core, mixed[HALF:], mixed[:HALF])
    last = copy(out_send, out_got, out_send_sem, out_recv, sibling)
    last.start()
    for one in to_sibling + to_block + to_pair:
        one.wait_send()
    arrived(key_z.at[pl.ds(0, 2 * side - 1)], keyz_send)
    arrived(key_y.at[pl.ds(0, side - 1)], keyy_send)
    sent(wbuf, w_send)
    sent(kvbuf, kv_send)
    last.wait()
    theirs = out_got[...]
    out_ref[:, : GQ * DH] = jnp.where(first_core, own_out, theirs)
    out_ref[:, GQ * DH :] = jnp.where(first_core, theirs, own_out)


def on_device(seq, byte_rows, norm_gain, key_weight, value_weight, pool_query, patch_starts):
    side = math.isqrt(seq // 2)
    rows, width = byte_rows.shape
    gathered = (side, side, 2, HALF, LANES)
    dma = pltpu.SemaphoreType.DMA
    scratch = [
        pltpu.VMEM((rows, width), bf16),
        pltpu.VMEM(norm_gain.shape, f32),
        pltpu.VMEM(key_weight.shape, bf16),
        pltpu.VMEM(value_weight.shape, bf16),
        pltpu.VMEM(pool_query.shape, f32),
        pltpu.VMEM(patch_starts.shape, jnp.int32),
        pltpu.VMEM(gathered, bf16),
        pltpu.VMEM(gathered, bf16),
        pltpu.VMEM((HALF, LANES), bf16),
        pltpu.VMEM((rows, width), bf16),
        pltpu.VMEM((2 * rows, width), bf16),
        pltpu.VMEM((4, 1, 128), jnp.int32),
        pltpu.VMEM((2, 1, 128), f32),
        pltpu.VMEM((2 * side, 1, 128), f32),
        pltpu.VMEM((side, side, 128), f32),
        pltpu.VMEM((2, 2 * HALF, width), bf16),
        pltpu.VMEM((2, 2 * HALF, width), f32),
        pltpu.VMEM((2 * HALF, width), bf16),
        pltpu.VMEM((8, 128), f32),
        pltpu.VMEM((8, 128), f32),
        pltpu.VMEM((6 * HALF, side * side * 2 * HALF), bf16),
        pltpu.VMEM((side * side, width), bf16),
        pltpu.VMEM((128, width), f32),
        pltpu.VMEM((4 * HALF, 2 * rows), f32),
        pltpu.VMEM((side * side * 2 * HALF // 128, min(256, width), 128), bf16),
        pltpu.VMEM((1, 2 * rows), f32),
        pltpu.VMEM((1, 2 * HALF * GQ), f32),
        pltpu.VMEM((1, 2 * HALF * GQ), f32),
        pltpu.VMEM((DH, 2 * HALF * GQ), f32),
        pltpu.VMEM((HALF, GQ * DH), bf16),
        pltpu.VMEM((HALF, GQ * DH), bf16),
        dma((6,)),
        dma((side, side, 2)),
        dma((side, side, 2)),
        dma((2,)),
        dma((4,)),
        dma(()),
        dma(()),
        dma((2,)),
        dma(()),
        dma((2, 2)),
        dma((2, 2)),
        dma((2,)),
        dma((3,)),
        dma(()),
        dma(()),
        dma((2,)),
        dma(()),
    ]
    return pl.pallas_call(
        functools.partial(kernel, side),
        out_shape=jax.ShapeDtypeStruct((HALF, 2 * GQ * DH), bf16),
        in_specs=[pl.BlockSpec(memory_space=pl.ANY)] * 6,
        out_specs=pl.BlockSpec(memory_space=pltpu.VMEM),
        scratch_shapes=scratch,
        compiler_params=pltpu.CompilerParams(
            collective_id=0, has_side_effects=True, vmem_limit_bytes=60 * 1024 * 1024
        ),
    )(byte_rows, norm_gain, key_weight, value_weight, pool_query, patch_starts)


def solution(mesh):
    return jax.shard_map(
        functools.partial(on_device, mesh.shape["seq"]),
        mesh=mesh,
        in_specs=(
            P(("dp", "seq"), None),
            P(),
            P("seq", "mp"),
            P("seq", "mp"),
            P("mp", None),
            P(("dp", "seq")),
        ),
        out_specs=P(("dp", "seq"), "mp"),
        check_vma=False,
    )
```

```python
import functools
import math

import jax
import jax.numpy as jnp
from jax import lax
from jax.experimental import pallas as pl
from jax.experimental.pallas import tpu as pltpu
from jax.sharding import PartitionSpec as P

DH = 128
GQ = 4
VW = 768
HALF = 32
LANES = 256
NEG = -1e30
MESH = pl.DeviceIdType.MESH
f32 = jnp.float32
bf16 = jnp.bfloat16


def iota(shape, dim):
    return lax.broadcasted_iota(jnp.int32, shape, dim)


def dot(a, b, dims=((1,), (0,))):
    return lax.dot_general(a, b, (dims, ((), ())), preferred_element_type=f32)


def kernel(
    side,
    bytes_in,
    gain_in,
    kw_in,
    vw_in,
    pq_in,
    starts_in,
    out_ref,
    bytes_ref,
    gain_ref,
    kw_ref,
    vw_ref,
    pq_ref,
    starts_ref,
    wbuf,
    kvbuf,
    wstage,
    sib_bytes,
    normed,
    starts_buf,
    key_stage,
    key_z,
    key_y,
    send_rows,
    own_rows,
    got_rows,
    send_stats,
    got_stats,
    spread,
    pick_ref,
    lane_ref,
    member_ref,
    choose_ref,
    score_ref,
    top_ref,
    total_ref,
    mix_ref,
    out_send,
    out_got,
    load_sem,
    w_recv,
    kv_recv,
    sib_recv,
    starts_recv,
    keyz_recv,
    keyy_recv,
    pair_recv,
    out_recv,
    w_send,
    kv_send,
    sib_send,
    starts_send,
    keyz_send,
    keyy_send,
    pair_send,
    out_send_sem,
):
    me = lax.axis_index("seq")
    core = lax.rem(me, 2)
    y = lax.rem(me // 2, side)
    z = me // (2 * side)
    chip = me // 2
    block_at = lax.rem(me, 4)
    pair_at = lax.rem(chip, 2)
    width = bytes_ref.shape[1]
    rows = bytes_ref.shape[0]

    def at(zz, yy, cc):
        return (zz * side + yy) * 2 + cc

    sibling = at(z, y, 1 - core)
    pair_y = y + 1 - 2 * pair_at
    pair = at(z, pair_y, core)
    cross = at(z, pair_y, 1 - core)

    def wrap(index):
        return lax.rem(index + 2 * side, side)

    def copy(src, dst, send_sem, recv_sem, target):
        return pltpu.make_async_remote_copy(
            src_ref=src,
            dst_ref=dst,
            send_sem=send_sem,
            recv_sem=recv_sem,
            device_id={"seq": target},
            device_id_type=MESH,
        )

    def arrived(ref, sem):
        pltpu.make_async_copy(ref, ref, sem).wait()

    loads = [
        pltpu.make_async_copy(src, dst, load_sem.at[k])
        for k, (src, dst) in enumerate(
            (
                (kw_in, kw_ref),
                (pq_in, pq_ref),
                (vw_in, vw_ref),
                (starts_in, starts_ref),
                (bytes_in, bytes_ref),
                (gain_in, gain_ref),
            )
        )
    ]
    for one in loads:
        one.start()

    barrier = pltpu.get_barrier_semaphore()

    def greet(target):
        pl.semaphore_signal(barrier, inc=1, device_id={"seq": target}, device_id_type=MESH)

    @pl.loop(1, side)
    def _(i):
        greet(at(wrap(z + i), y, core))
        greet(at(wrap(z + i), y, 1 - core))
        greet(at(z, wrap(y + i), core))

    greet(sibling)
    greet(cross)

    for one in loads[:2]:
        one.wait()
    folded = kw_ref[...].astype(f32)
    depth = folded.shape[0]
    row_at = iota((depth, 128), 0)
    lane_at = iota((depth, 128), 1)
    for head in range(2):
        col = jnp.sum(folded[:, head * DH : (head + 1) * DH] * pq_ref[head : head + 1, :], axis=1, keepdims=True)
        key_stage[head] = jnp.sum(jnp.where(lane_at == row_at + core * 16, col, 0.0), axis=0, keepdims=True)
    key_z[z * 2 + core] = key_stage[core]

    loads[2].wait()
    part = vw_ref[...].astype(f32)
    first_core = core == 0
    pieces = []
    for head in range(2):
        cuts = [part[:, head * VW + n * LANES : head * VW + (n + 1) * LANES] for n in range(VW // LANES)]
        cuts.append(jnp.zeros((HALF - depth * len(cuts), LANES), f32))
        pieces.append(jnp.concatenate(cuts, axis=0).astype(bf16))
    wbuf[z, y, core] = jnp.where(first_core, pieces[0], pieces[1])
    wstage[...] = jnp.where(first_core, pieces[1], pieces[0])

    loads[3].wait()
    starts_buf[block_at] = jnp.concatenate(
        [starts_ref[...].reshape(1, HALF), jnp.zeros((1, 128 - HALF), jnp.int32)], axis=1
    )

    pl.semaphore_wait(barrier, 3 * side - 1)

    def ref_of(buf, half, a, b):
        return buf.at[a, b, 0] if half == 0 else buf.at[b, a, 1]

    def dev_of(half, a, b):
        return at(a, b, core) if half == 0 else at(b, a, core)

    def own_of(half):
        return (z, y) if half == 0 else (y, z)

    def sem_of(sems, half, a, b):
        return sems.at[a, b, 0] if half == 0 else sems.at[b, a, 1]

    def ring(buf, recv, send, half, a, b, step):
        a0, b0 = own_of(half)
        ref = ref_of(buf, half, a, b)
        copy(
            ref, ref, send.at[half, 1], sem_of(recv, half, a, b), dev_of(half, a0, wrap(b0 + step))
        ).start()

    def pass_on(buf, recv, send, half, a, b, step, distance, even):
        last = distance == side // 2 - 1
        if not last or even == (step == 1):
            ring(buf, recv, send, half, a, b, step)

    def begin(buf, recv, send, half):
        a0, b0 = own_of(half)
        ref = ref_of(buf, half, a0, b0)
        for step in (1, -1):
            pass_on(buf, recv, send, half, a0, b0, step, 0, True)

        @pl.loop(1, side)
        def _(i):
            copy(
                ref, ref, send.at[half, 0], sem_of(recv, half, a0, b0), dev_of(half, wrap(a0 + i), b0)
            ).start()

    def visit(buf, recv, send, distance, t, halves=(0, 1)):
        for half in halves:
            a0, b0 = own_of(half)
            for even, a in ((True, wrap(a0 - t)), (False, wrap(a0 + t + 1))):
                if distance == 0:

                    def take(half=half, a=a, b0=b0, even=even):
                        arrived(ref_of(buf, half, a, b0), sem_of(recv, half, a, b0))
                        for step in (1, -1):
                            pass_on(buf, recv, send, half, a, b0, step, 0, even)

                    if even:
                        pl.when(t > 0)(take)
                    else:
                        take()
                elif distance < side // 2:
                    for step in (1, -1):
                        b = wrap(b0 - step * distance)
                        arrived(ref_of(buf, half, a, b), sem_of(recv, half, a, b))
                        pass_on(buf, recv, send, half, a, b, step, distance, even)
                else:
                    b = wrap(b0 + distance)
                    arrived(ref_of(buf, half, a, b), sem_of(recv, half, a, b))

    def stage(buf, recv, send, distance):
        @pl.loop(0, side // 2)
        def _(t):
            visit(buf, recv, send, distance, t)

    def sent(buf, send):
        for half in (0, 1):
            ref = buf.at[0, pl.ds(0, side - 1), half]
            arrived(ref, send.at[half, 0])
            ref = buf.at[:, pl.ds(0, side - 1), half]
            arrived(ref, send.at[half, 1])

    weights = (wbuf, w_recv, w_send)
    sib_piece = wbuf.at[z, y, 1 - core]
    chips = side * side
    half_rows = 2 * HALF
    window = min(256, width)
    blocks = side * side * 2 * HALF // 128
    lefts = [min(4 * depth * b // 128 * 128, width - window) for b in range(blocks)]

    def send_keys():
        def keys_to(target, head):
            copy(key_stage.at[head], key_z.at[z * 2 + core], keyz_send, keyz_recv, target).start()

        @pl.loop(1, side)
        def _(i):
            for head in range(2):
                keys_to(at(wrap(z + i), y, head), head)

        keys_to(sibling, 1 - core)

    def send_piece():
        to_sibling[0].start()

    def send_bytes():
        loads[4].wait()
        to_sibling[1].start()

    def send_starts():
        for one in to_block:
            one.start()

    def begin_weights():
        @pl.when(first_core)
        def _():
            begin(*weights, 0)
            arrived(sib_piece, sib_recv.at[0])
            begin(*weights, 1)

        @pl.when(core == 1)
        def _():
            begin(*weights, 1)
            arrived(sib_piece, sib_recv.at[0])
            begin(*weights, 0)

    def norm_rows(ref, first, quarter):
        @pl.loop(quarter * rows // 128, (quarter + 1) * rows // 128)
        def _(i):
            at_row = pl.multiple_of(i * 32, 32)
            wide = ref[pl.ds(at_row, 32), :].astype(f32)
            scale = lax.rsqrt(jnp.mean(wide * wide, axis=-1, keepdims=True) + 1e-05)
            normed[pl.ds(pl.multiple_of(first + at_row, 32), 32), :] = (
                wide * scale * gain_ref[...].reshape(1, width)
            ).astype(bf16)

    def norm_own(quarter):
        if quarter == 0:
            loads[5].wait()
        norm_rows(bytes_ref, core * rows, quarter)

    def norm_sibling(quarter):
        if quarter == 0:
            arrived(sib_bytes, sib_recv.at[1])
        norm_rows(sib_bytes, (1 - core) * rows, quarter)

    def pass_keys():
        arrived(key_z.at[pl.ds(0, 2 * side - 1)], keyz_recv)
        key_y[y] = jnp.concatenate([key_z[2 * i] + key_z[2 * i + 1] for i in range(side)], axis=0)

        @pl.loop(1, side)
        def _(i):
            copy(key_y.at[y], key_y.at[y], keyy_send, keyy_recv, at(z, wrap(y + i), core)).start()

    def make_pick():
        column = iota((1, width), 1)
        column_chip = column // (2 * depth)
        column_row = lax.rem(column_chip, side) * side + column_chip // side
        pick_ref[...] = jnp.where(iota((chips, width), 0) == column_row, 1.0, 0.0).astype(bf16)
        column_lane = lax.rem(column // depth, 2) * 16 + lax.rem(column, depth)
        lane_row = iota((128, width), 0)
        lane_ref[...] = jnp.where(lax.rem(lane_row, 32) == column_lane, 1.0, 0.0)

    def make_member():
        for k in range(1, 4):
            other = lax.rem(block_at + k, 4)
            arrived(starts_buf.at[other], starts_recv.at[other])
        patch_sub = iota((HALF, 128), 0)
        patch_lane = iota((HALF, 128), 1)
        first_cols, next_cols = [], []
        for q in range(4):
            row = starts_buf[q]
            follow = (chip // 2 + 1) * (4 * rows) if q == 3 else starts_buf[q + 1][:, 0:1]
            row = jnp.where(iota((1, 128), 1) == HALF, follow, row)
            first_cols.append(jnp.sum(jnp.where(patch_lane == patch_sub, row, 0), axis=1, keepdims=True))
            next_cols.append(jnp.sum(jnp.where(patch_lane == patch_sub + 1, row, 0), axis=1, keepdims=True))
        first_col = jnp.concatenate(first_cols, axis=0)
        next_col = jnp.concatenate(next_cols, axis=0)
        position = chip * (2 * rows) + iota((1, 2 * rows), 1)
        member_ref[...] = jnp.where((first_col <= position) & (position < next_col), 1.0, 0.0)

    def make_choose():
        lane = iota((1, 128), 1)
        in_piece = lax.rem(lane, HALF)
        source = jnp.where(in_piece < 3 * depth, (lane // HALF) * depth + lax.rem(in_piece, depth), -100000)
        sub = iota((window, 128), 0)
        for b in range(blocks):
            choose_ref[b] = jnp.where(sub == source + (4 * depth * b - lefts[b]), 1.0, 0.0).astype(bf16)

    def score():
        arrived(key_y.at[pl.ds(0, side - 1)], keyy_recv)
        table = key_y[...].reshape(chips, 128)
        high = table.astype(bf16).astype(f32)
        middle = (table - high).astype(bf16).astype(f32)
        low = (table - high - middle).astype(bf16).astype(f32)
        packed = (high + pltpu.roll(middle, 32, axis=1) + pltpu.roll(low, 64, axis=1)).astype(bf16)
        taken = dot(packed, pick_ref[...], ((0,), (0,)))
        key_rows = (taken * lane_ref[...]).astype(bf16)
        score_ref[...] = jnp.sum(dot(key_rows, normed[...], ((1,), (1,))), axis=0, keepdims=True) / math.sqrt(DH)

    def pool():
        member = member_ref[...] > 0.5
        masked = jnp.where(member, score_ref[...], NEG)
        top = jnp.max(masked, axis=1, keepdims=True)
        weight = jnp.where(member, jnp.exp(masked - top), 0.0).astype(bf16)
        total = jnp.sum(weight.astype(f32), axis=1, keepdims=True)
        share = jnp.where(total > 0.0, 1.0 / jnp.maximum(total, 1e-30), 0.0)
        pooled_rows = dot(weight, normed[...]) * share
        own_rows[...] = pooled_rows.reshape(2, half_rows, width)
        send_rows[...] = pooled_rows.astype(bf16).reshape(2, half_rows, width)
        to_pair[0].start()
        eye = iota((4 * HALF, 128), 0) == iota((4 * HALF, 128), 1)
        top_row = jnp.sum(jnp.where(eye, top, 0.0), axis=0, keepdims=True)
        total_row = jnp.sum(jnp.where(eye, total, 0.0), axis=0, keepdims=True)
        send_stats[...] = jnp.concatenate([top_row, total_row, jnp.zeros((6, 128), f32)], axis=0)
        to_pair[1].start()

    def merge():
        to_pair[1].wait_recv()
        eye = iota((half_rows, 128), 1) == iota((half_rows, 128), 0) + pair_at * half_rows

        def to_column(row):
            return jnp.sum(jnp.where(eye, row, 0.0), axis=1, keepdims=True)

        own_top, own_total = to_column(send_stats[0:1, :]), to_column(send_stats[1:2, :])
        got_top, got_total = to_column(got_stats[0:1, :]), to_column(got_stats[1:2, :])
        top = jnp.maximum(own_top, got_top)
        own_part = jnp.exp(own_top - top) * own_total
        got_part = jnp.exp(got_top - top) * got_total
        share = 1.0 / (own_part + got_part)
        to_pair[0].wait_recv()
        merged = own_rows[pair_at] * (own_part * share) + got_rows[...].astype(f32) * (got_part * share)
        merged = merged.astype(bf16)
        which = lax.rem(iota((1, 128), 1), HALF) // depth
        for b in range(blocks):
            block = dot(merged[:, lefts[b] : lefts[b] + window], choose_ref[b])
            for n in range(3):
                spread[n * half_rows : (n + 1) * half_rows, b * 128 : (b + 1) * 128] = jnp.where(
                    which == n, block, 0.0
                ).astype(bf16)

    to_sibling = [
        copy(wstage, wbuf.at[z, y, core], sib_send.at[0], sib_recv.at[0], sibling),
        copy(bytes_ref, sib_bytes, sib_send.at[1], sib_recv.at[1], sibling),
    ]
    to_block = [
        copy(starts_buf.at[block_at], starts_buf.at[block_at], starts_send.at[k], starts_recv.at[block_at], target)
        for k, target in enumerate((sibling, pair, cross))
    ]
    to_pair = [
        copy(send_rows.at[1 - pair_at], got_rows, pair_send.at[0], pair_recv.at[0], pair),
        copy(send_stats, got_stats, pair_send.at[1], pair_recv.at[1], pair),
    ]
    send_keys()
    send_piece()
    send_starts()
    send_bytes()
    begin_weights()
    norm_own(0)
    norm_own(1)
    norm_own(2)
    norm_own(3)
    pass_keys()
    stage(*weights, 0)
    norm_sibling(0)
    norm_sibling(1)
    norm_sibling(2)
    norm_sibling(3)
    stage(*weights, 1)
    make_pick()
    make_member()
    visit(*weights, 2, 0)
    visit(*weights, 2, 1)
    score()
    visit(*weights, 2, 2)
    visit(*weights, 2, 3)
    pool()
    stage(*weights, 3)
    make_choose()
    merge()
    stage(*weights, 4)
    span = side * 2 * HALF

    def mapped(low, high):
        total = jnp.zeros(((high - low) * half_rows, LANES), f32)
        for zz in range(side):
            total = total + dot(
                spread[low * half_rows : high * half_rows, zz * span : (zz + 1) * span],
                wbuf[zz].reshape(span, LANES),
            )
        return total.astype(bf16)

    patches = (kvbuf, kv_recv, kv_send)
    kvbuf[z, y] = mapped(2, 3).reshape(2, HALF, LANES)
    begin(*patches, 0)
    begin(*patches, 1)
    mapped_queries = mapped(0, 2)
    queries = jnp.concatenate(
        [mapped_queries[n * half_rows : (n + 1) * half_rows, k * DH : (k + 1) * DH] for n in range(2) for k in range(2)],
        axis=0,
    )

    query_at = chip * half_rows + lax.rem(iota((1, GQ * half_rows), 1), half_rows)
    key_index = iota((side * HALF, 1), 0)
    top_ref[...] = jnp.full(top_ref.shape, NEG, f32)
    total_ref[...] = jnp.zeros(total_ref.shape, f32)
    mix_ref[...] = jnp.zeros(mix_ref.shape, f32)

    def attend(half, b):
        if half == 0:
            pair_of = kvbuf[:, b, 0]
            key_at = (key_index // HALF * side + b) * half_rows
        else:
            pair_of = kvbuf[b, :, 1]
            key_at = (key_index // HALF + b * side) * half_rows + HALF
        pair_of = pair_of.reshape(side * HALF, LANES)
        logits = dot(pair_of[:, :DH], queries, ((1,), (1,))) / math.sqrt(DH)
        logits = jnp.where(key_at + lax.rem(key_index, HALF) <= query_at, logits, NEG)
        old = top_ref[...]
        new = jnp.maximum(old, jnp.max(logits, axis=0, keepdims=True))
        raised = jnp.exp(logits - new)
        keep = jnp.exp(old - new)
        top_ref[...] = new
        total_ref[...] = total_ref[...] * keep + jnp.sum(raised, axis=0, keepdims=True)
        mix_ref[...] = mix_ref[...] * keep + dot(pair_of[:, DH:], raised.astype(bf16), ((0,), (0,)))

    def ready_at(distance):
        for half in (0, 1):
            b0 = own_of(half)[1]
            if distance == 0:
                yield half, b0
            else:
                yield half, wrap(b0 + distance)
                yield half, wrap(b0 - distance)

    queue = []
    for distance in range(side // 2):
        for t in range(side // 2):
            visit(*patches, distance, t)
            if queue:
                attend(*queue.pop(0))
        queue += list(ready_at(distance))
    for half in (0, 1):
        for t in range(side // 2):
            visit(*patches, side // 2, t, (half,))
            if queue:
                attend(*queue.pop(0))
        attend(half, wrap(own_of(half)[1] + side // 2))

    mixed = (mix_ref[...] / total_ref[...]).T
    mixed = jnp.concatenate([mixed[h * half_rows : (h + 1) * half_rows] for h in range(GQ)], axis=1).astype(bf16)
    own_out = jnp.where(first_core, mixed[:HALF], mixed[HALF:])
    out_send[...] = jnp.where(first_core, mixed[HALF:], mixed[:HALF])
    last = copy(out_send, out_got, out_send_sem, out_recv, sibling)
    last.start()
    for one in to_sibling + to_block + to_pair:
        one.wait_send()
    arrived(key_z.at[pl.ds(0, 2 * side - 1)], keyz_send)
    arrived(key_y.at[pl.ds(0, side - 1)], keyy_send)
    sent(wbuf, w_send)
    sent(kvbuf, kv_send)
    last.wait()
    theirs = out_got[...]
    out_ref[:, : GQ * DH] = jnp.where(first_core, own_out, theirs)
    out_ref[:, GQ * DH :] = jnp.where(first_core, theirs, own_out)


def on_device(seq, byte_rows, norm_gain, key_weight, value_weight, pool_query, patch_starts):
    side = math.isqrt(seq // 2)
    rows, width = byte_rows.shape
    gathered = (side, side, 2, HALF, LANES)
    dma = pltpu.SemaphoreType.DMA
    scratch = [
        pltpu.VMEM((rows, width), bf16),
        pltpu.VMEM(norm_gain.shape, f32),
        pltpu.VMEM(key_weight.shape, bf16),
        pltpu.VMEM(value_weight.shape, bf16),
        pltpu.VMEM(pool_query.shape, f32),
        pltpu.VMEM(patch_starts.shape, jnp.int32),
        pltpu.VMEM(gathered, bf16),
        pltpu.VMEM(gathered, bf16),
        pltpu.VMEM((HALF, LANES), bf16),
        pltpu.VMEM((rows, width), bf16),
        pltpu.VMEM((2 * rows, width), bf16),
        pltpu.VMEM((4, 1, 128), jnp.int32),
        pltpu.VMEM((2, 1, 128), f32),
        pltpu.VMEM((2 * side, 1, 128), f32),
        pltpu.VMEM((side, side, 128), f32),
        pltpu.VMEM((2, 2 * HALF, width), bf16),
        pltpu.VMEM((2, 2 * HALF, width), f32),
        pltpu.VMEM((2 * HALF, width), bf16),
        pltpu.VMEM((8, 128), f32),
        pltpu.VMEM((8, 128), f32),
        pltpu.VMEM((6 * HALF, side * side * 2 * HALF), bf16),
        pltpu.VMEM((side * side, width), bf16),
        pltpu.VMEM((128, width), f32),
        pltpu.VMEM((4 * HALF, 2 * rows), f32),
        pltpu.VMEM((side * side * 2 * HALF // 128, min(256, width), 128), bf16),
        pltpu.VMEM((1, 2 * rows), f32),
        pltpu.VMEM((1, 2 * HALF * GQ), f32),
        pltpu.VMEM((1, 2 * HALF * GQ), f32),
        pltpu.VMEM((DH, 2 * HALF * GQ), f32),
        pltpu.VMEM((HALF, GQ * DH), bf16),
        pltpu.VMEM((HALF, GQ * DH), bf16),
        dma((6,)),
        dma((side, side, 2)),
        dma((side, side, 2)),
        dma((2,)),
        dma((4,)),
        dma(()),
        dma(()),
        dma((2,)),
        dma(()),
        dma((2, 2)),
        dma((2, 2)),
        dma((2,)),
        dma((3,)),
        dma(()),
        dma(()),
        dma((2,)),
        dma(()),
    ]
    return pl.pallas_call(
        functools.partial(kernel, side),
        out_shape=jax.ShapeDtypeStruct((HALF, 2 * GQ * DH), bf16),
        in_specs=[pl.BlockSpec(memory_space=pl.ANY)] * 6,
        out_specs=pl.BlockSpec(memory_space=pltpu.VMEM),
        scratch_shapes=scratch,
        compiler_params=pltpu.CompilerParams(
            collective_id=0, has_side_effects=True, vmem_limit_bytes=54800 * 1024
        ),
    )(byte_rows, norm_gain, key_weight, value_weight, pool_query, patch_starts)


def solution(mesh):
    return jax.shard_map(
        functools.partial(on_device, mesh.shape["seq"]),
        mesh=mesh,
        in_specs=(
            P(("dp", "seq"), None),
            P(),
            P("seq", "mp"),
            P("seq", "mp"),
            P("mp", None),
            P(("dp", "seq")),
        ),
        out_specs=P(("dp", "seq"), "mp"),
        check_vma=False,
    )
```
